128 devices in a mesh: tm: 8 (over y_lo, x), row: 4 (over z), col: 4 (over y_hi, core).
Axes of the slice: x: 4, y: 4 (y_hi: 2, y_lo: 2; y = y_hi * 2 + y_lo), z: 4, core: 2. Of those that a mesh axis runs over, the one named last changes fastest.
Arguments:
- tokens: bfloat16 [16, 64, 96, 384], P('tm', 'row', 'col'), may hold values from -8 to 8
- cache_first: bfloat16 [2, 64, 96, 384], P(None, 'row', 'col'), may hold values from -0.25 to 1.5
- cache_second: bfloat16 [2, 64, 96, 384], P(None, 'row', 'col'), may hold values from -0.25 to 1.5
- gain_first: float32 [384], replicated, may hold values from 0.1 to 1.9
- gain_second: float32 [384], replicated, may hold values from 0.1 to 1.9
- conv_first: bfloat16 [3, 3, 3, 384, 384], replicated, may hold values from -0.0625 to 0.0625
- conv_second: bfloat16 [3, 3, 3, 384, 384], replicated, may hold values from -0.0625 to 0.0625
- gain_attn: float32 [384], replicated, may hold values from 0.1 to 1.9
- query_weight: bfloat16 [384, 384], replicated, may hold values from -8 to 8
- key_weight: bfloat16 [384, 384], replicated, may hold values from -8 to 8
- value_weight: bfloat16 [384, 384], replicated, may hold values from -0.4375 to 0.4375
- out_weight: bfloat16 [384, 384], replicated, may hold values from -0.3125 to 0.3125
Outputs:
- decoded: bfloat16 [16, 64, 96, 384], P('tm', 'row', 'col')
The draws below stay inside these ranges and needn't reach their ends.
All inputs are finite; a program needn't handle non-finite values.
Results may differ from the reference program's by a relative error of at most 0.019.
Values may be sent and summed in bfloat16 or wider, within the bound.
A program may use at most 128 MiB of HBM per device.

```python
import jax
import jax.numpy as jnp
from jax import lax

C = 384
TF = 16
H = 64
W = 96


def draw_tokens(key, part):
    noise_key = jax.random.fold_in(key, 1)
    base = jax.random.normal(noise_key, (TF, H, W, C), jnp.float32)
    return jnp.clip(base, -8.0, 8.0).astype(jnp.bfloat16)


def draw_query_weight(key, part):
    own_key = jax.random.fold_in(key, 3)
    mixed = jax.random.normal(own_key, (C, C), jnp.float32) * (2.0 * C ** (-0.5))
    return jnp.clip(mixed, -8.0, 8.0).astype(jnp.bfloat16)


def draw_key_weight(key, part):
    own_key = jax.random.fold_in(key, 4)
    mixed = jax.random.normal(own_key, (C, C), jnp.float32) * (2.0 * C ** (-0.5))
    return jnp.clip(mixed, -8.0, 8.0).astype(jnp.bfloat16)


def levels(stream_key, dims, split, low, high):
    loudness = 1.0
    for axis_at, blocks in split:
        draws = jax.random.uniform(jax.random.fold_in(jax.random.fold_in(stream_key, 6), axis_at), (blocks,), jnp.float32, low / len(split), high / len(split))
        loudness = loudness * jnp.repeat(jnp.exp(draws), dims[axis_at] // blocks).reshape((-1,) + (1,) * (len(dims) - 1 - axis_at))
    return loudness


def bell_draw(stream_key, extent, scale, bound, held_as=jnp.bfloat16):
    values = jax.random.normal(stream_key, extent, jnp.float32) * scale
    return jnp.minimum(jnp.maximum(values, -bound), bound).astype(held_as)


def setup_inputs(seed: int = 0) -> dict:
    key_of = jax.random.split(jax.random.key(seed), 13)
    return {
        "tokens": draw_tokens(jax.random.fold_in(key_of[12], 71), 0),
        "cache_first": jnp.clip(-0.25 + 1.75 * jax.random.uniform(key_of[1], (2, H, W, C), jnp.float32) ** levels(key_of[1], (2, H, W, C), ((1, 4), (2, 4)), -0.2, 0.2), -0.25, 1.5).astype(jnp.bfloat16),
        "cache_second": jnp.clip(-0.25 + 1.75 * jax.random.uniform(key_of[2], (2, H, W, C), jnp.float32) ** levels(key_of[2], (2, H, W, C), ((1, 4), (2, 4)), -0.2, 0.2), -0.25, 1.5).astype(jnp.bfloat16),
        "gain_first": jnp.clip(1.0 + 0.18 * jax.random.normal(key_of[3], (C,), jnp.float32), 0.1, 1.9),
        "gain_second": jnp.clip(1.0 + 0.18 * jax.random.normal(key_of[4], (C,), jnp.float32), 0.1, 1.9),
        "conv_first": bell_draw(key_of[5], (3, 3, 3, C, C), (27 * C) ** -0.5, 0.0625),
        "conv_second": bell_draw(key_of[6], (3, 3, 3, C, C), (27 * C) ** -0.5, 0.0625),
        "gain_attn": jnp.clip(1.0 + 0.18 * jax.random.normal(key_of[7], (C,), jnp.float32), 0.1, 1.9),
        "query_weight": draw_query_weight(jax.random.fold_in(key_of[12], 71), 0),
        "key_weight": draw_key_weight(jax.random.fold_in(key_of[12], 71), 0),
        "value_weight": bell_draw(key_of[10], (C, C), (C // 2) ** -0.5, 0.4375),
        "out_weight": bell_draw(key_of[11], (C, C), C ** -0.5, 0.3125),
    }


def norm_gain(v, gain):
    return v * lax.rsqrt(lax.optimization_barrier(jnp.mean(v * v, axis=-1, keepdims=True)) + 1e-06) * gain.astype(jnp.float32)

def causal_conv(frames, cache, kernel):
    whole = jnp.concatenate([cache, frames], axis=0).astype(jnp.float32)
    result = lax.conv_general_dilated(whole[None], kernel.astype(jnp.float32), (1, 1, 1), [(0, 0), (1, 1), (1, 1)], dimension_numbers=('NDHWC', 'DHWIO', 'NDHWC'), precision=lax.Precision.HIGHEST)
    return result[0]

def reference(tokens, cache_first, cache_second, gain_first, gain_second, conv_first, conv_second, gain_attn, query_weight, key_weight, value_weight, out_weight):
    chans = tokens.shape[-1]
    source = tokens.astype(jnp.float32)
    first_input = jax.nn.silu(norm_gain(source, gain_first)).astype(jnp.bfloat16)
    first_out = causal_conv(first_input, cache_first, conv_first)
    second_input = jax.nn.silu(norm_gain(first_out, gain_second)).astype(jnp.bfloat16)
    second_out = causal_conv(second_input, cache_second, conv_second)
    stream = (source + second_out).astype(jnp.bfloat16)
    normed = norm_gain(stream.astype(jnp.float32), gain_attn).astype(jnp.bfloat16)
    flat = normed.reshape(-1, chans)
    query = jnp.dot(flat, query_weight, preferred_element_type=jnp.float32).astype(jnp.bfloat16).reshape(TF, H * W, chans)
    keys = jnp.dot(flat, key_weight, preferred_element_type=jnp.float32).astype(jnp.bfloat16).reshape(TF, H * W, chans)
    values = jnp.dot(flat, value_weight, preferred_element_type=jnp.float32).astype(jnp.bfloat16).reshape(TF, H * W, chans)
    scale = chans ** (-0.5)

    def one_frame(items):
        qf, kf, vf = items
        scores = jnp.dot(qf, kf.T, preferred_element_type=jnp.float32) * scale
        top = lax.optimization_barrier(jnp.max(scores, axis=-1, keepdims=True))
        expo = jnp.exp(scores - top)
        weights = expo.astype(jnp.bfloat16)
        mixed = jnp.dot(weights, vf, preferred_element_type=jnp.float32)
        return (mixed / lax.optimization_barrier(jnp.sum(expo, axis=-1, keepdims=True))).astype(jnp.bfloat16)
    attended = lax.map(one_frame, (query, keys, values))
    projected = jnp.dot(attended.reshape(-1, chans), out_weight, preferred_element_type=jnp.float32)
    decoded = stream.astype(jnp.float32) + projected.reshape(TF, H, W, chans)
    return decoded.astype(jnp.bfloat16)
```

```python
import functools
import math

import jax
import jax.numpy as jnp
from jax import lax
from jax.experimental import pallas as pl
from jax.experimental.pallas import tpu as pltpu
from jax.sharding import PartitionSpec as P

MESH = pl.DeviceIdType.MESH
F32 = jnp.float32
BF16 = jnp.bfloat16
C = 384
SIDES = [(dr, dc) for dr in (-1, 0, 1) for dc in (-1, 0, 1) if (dr, dc) != (0, 0)]
TILE = 8


def normed_by(v, gain):
    return v * lax.rsqrt(jnp.mean(v * v, axis=-1, keepdims=True) + 1e-06) * gain


def silu(v):
    return v / (1.0 + jnp.exp(-v))


def conv_kernel(
    tok, cache1, cache2, gain1, gain2, gain_a, w1, w2,
    stream_out, normed_out,
    wbuf, views, lift, held, acc, edges, cache_edges, halo_c, halo_r, halo_k, halo_t,
    w_sem, send_sem, recv_sem,
):
    ntm, nrow, ncol = (lax.axis_size(a) for a in ("tm", "row", "col"))
    tm, row, col = (lax.axis_index(a) for a in ("tm", "row", "col"))
    cols, rows = tok.shape[1], tok.shape[2]
    flat = cols * rows

    weights = []
    for stage, src in ((0, w1), (1, w2)):
        for a in (2, 1, 0):
            for c in range(3):
                copy = pltpu.make_async_copy(
                    src.at[a, :, c], wbuf.at[stage, a, c], w_sem.at[stage, a]
                )
                copy.start()
                weights.append((stage, a, copy))

    def wait_weights(stage, a):
        for s, b, copy in weights:
            if (s, b) == (stage, a):
                copy.wait()

    def there(dr, dc):
        ok = (row + dr >= 0) & (row + dr < nrow)
        return ok & (col + dc >= 0) & (col + dc < ncol)

    barrier = pltpu.get_barrier_semaphore()
    for dr, dc in SIDES:
        @pl.when(there(dr, dc))
        def _():
            pl.semaphore_signal(barrier, inc=1, device_id=(tm, row + dr, col + dc), device_id_type=MESH)

        @pl.when(there(dr, dc) & (tm > 0))
        def _():
            pl.semaphore_signal(barrier, inc=1, device_id=(tm - 1, row + dr, col + dc), device_id_type=MESH)

    @pl.when(tm > 0)
    def _():
        pl.semaphore_signal(barrier, inc=1, device_id=(tm - 1, row, col), device_id_type=MESH)

    def as_int(flag):
        return jnp.where(flag, 1, 0)

    around = (1 + as_int(row > 0) + as_int(row < nrow - 1)) * (1 + as_int(col > 0) + as_int(col < ncol - 1))
    expected = around - 1 + jnp.where(tm < ntm - 1, around, 0)

    def side_parts(ref_tile, ref_edge, dr, dc):
        if dr == 0:
            return ref_tile.at[:, cols - 1 if dc == 1 else 0]
        line = 1 if dr == 1 else 0
        if dc == 0:
            return ref_edge.at[:, line]
        return ref_edge.at[:, line, pl.ds(16 if dc == 1 else 0, 16)]

    def landing(stage, pair, dr, dc):
        if dr == 0:
            return halo_c.at[stage, pair, :, 0 if dc == 1 else 1]
        top = 0 if dr == 1 else 1
        if dc == 0:
            return halo_r.at[stage, pair, :, top]
        return halo_k.at[stage, pair, :, top, 0 if dc == 1 else 1]

    def side_copy(stage, group, k, ref_tile, ref_edge, target):
        dr, dc = SIDES[k]
        pair = 1 if group == 0 else 0
        return pltpu.make_async_remote_copy(
            src_ref=side_parts(ref_tile, ref_edge, dr, dc),
            dst_ref=landing(stage, pair, dr, dc),
            send_sem=send_sem.at[stage, group, k],
            recv_sem=recv_sem.at[stage, pair, k],
            device_id=(target, row + dr, col + dc),
            device_id_type=MESH,
        )

    def tile_copy(stage):
        return pltpu.make_async_remote_copy(
            src_ref=held.at[stage],
            dst_ref=halo_t.at[stage],
            send_sem=send_sem.at[stage, 1, TILE],
            recv_sem=recv_sem.at[stage, 0, TILE],
            device_id=(tm + 1, row, col),
            device_id_type=MESH,
        )

    def all_sends(stage, act):
        cache = (cache1, cache2)[stage]

        @pl.when(tm < ntm - 1)
        def _():
            act(tile_copy(stage))

        for k, (dr, dc) in enumerate(SIDES):
            @pl.when(there(dr, dc))
            def _():
                act(side_copy(stage, 0, k, held.at[stage], edges.at[stage], tm))

            @pl.when(there(dr, dc) & (tm < ntm - 1))
            def _():
                act(side_copy(stage, 1, k, held.at[stage], edges.at[stage], tm + 1))

    def cache_sends(stage, act):
        cache = (cache1, cache2)[stage]
        for k, (dr, dc) in enumerate(SIDES):
            @pl.when(there(dr, dc) & (tm == 0))
            def _():
                act(side_copy(stage, 2, k, cache, cache_edges.at[stage], 0))

    def wait_sides(stage, pair):
        for k, (dr, dc) in enumerate(SIDES):
            @pl.when(there(-dr, -dc))
            def _():
                side_copy(stage, 1 - pair, k, held.at[stage], edges.at[stage], tm).wait_recv()

    def take_edges(src, dst):
        for i in range(2):
            for line, at in ((0, 0), (1, rows - 1)):
                dst[i, line, 0:cols, :] = lift[1:cols + 1, 8 + at, :].astype(BF16)

    def lift_tile(src):
        def step(j, _):
            lift[j + 1, 8:8 + rows, :] = src[j].astype(F32)
            return 0
        lax.fori_loop(0, cols, step, 0)

    def edges_of(src, dst, i):
        lift_tile(src)
        dst[i, 0, 0:cols, :] = lift[1:cols + 1, 8, :].astype(BF16)
        dst[i, 1, 0:cols, :] = lift[1:cols + 1, 8 + rows - 1, :].astype(BF16)

    def build(stage, pair, i, src):
        slot = 2 * pair + i
        lift_tile(src)
        lift[0, 8:8 + rows, :] = halo_c[stage, pair, i, 0].astype(F32)
        lift[cols + 1, 8:8 + rows, :] = halo_c[stage, pair, i, 1].astype(F32)
        for top, at in ((0, 7), (1, 8 + rows)):
            lift[1:cols + 1, at, :] = halo_r[stage, pair, i, top, 0:cols, :].astype(F32)
            lift[0, at, :] = halo_k[stage, pair, i, top, 0].astype(F32)[cols - 17]
            lift[cols + 1, at, :] = halo_k[stage, pair, i, top, 1].astype(F32)[0]

        def step(j, _):
            for b in range(3):
                views[slot, j, :, b * C:(b + 1) * C] = lift[j, 7 + b:7 + b + rows, :].astype(BF16)
            return 0
        lax.fori_loop(0, cols + 2, step, 0)

    def taps(stage, frame, first, last):
        parts = [
            views[frame + a, c:c + cols].reshape(flat, 3 * C)
            for a in range(first, last) for c in range(3)
        ]
        left = jnp.concatenate(parts, axis=1) if len(parts) > 1 else parts[0]
        right = wbuf[stage, first:last].reshape((last - first) * 9 * C, C)
        return jnp.dot(left, right, preferred_element_type=F32)

    def conv(stage):
        wait_sides(stage, 1)
        for i in range(2):
            build(stage, 1, i, held.at[stage, i])
        wait_weights(stage, 2)
        wait_weights(stage, 1)
        acc[0] = taps(stage, 0, 2, 3)
        acc[1] = taps(stage, 1, 1, 3)

        @pl.when(tm > 0)
        def _():
            tile_copy(stage).wait_recv()

        wait_sides(stage, 0)
        for i in range(2):
            build(stage, 0, i, halo_t.at[stage, i])
        wait_weights(stage, 0)
        acc[0] += taps(stage, 0, 0, 2)
        acc[1] += taps(stage, 1, 0, 1)

    for k, (dr, dc) in enumerate(SIDES):
        @pl.when(jnp.logical_not(there(-dr, -dc)))
        def _():
            for stage in range(2):
                for pair in range(2):
                    ref = landing(stage, pair, dr, dc)
                    ref[...] = jnp.zeros(ref.shape, BF16)
    for ref in (edges, cache_edges):
        for stage in range(2):
            for i in range(2):
                for line in range(2):
                    ref[stage, i, line, 16:32, :] = jnp.zeros((16, C), BF16)

    @pl.when(tm == 0)
    def _():
        for stage, cache in ((0, cache1), (1, cache2)):
            for i in range(2):
                halo_t[stage, i] = cache[i]
                edges_of(cache.at[i], cache_edges.at[stage], i)

    def first(j, _):
        for i in range(2):
            v = tok[i, pl.ds(2 * j, 2)].astype(F32)
            held[0, i, pl.ds(2 * j, 2)] = silu(normed_by(v, gain1[...])).astype(BF16)
        return 0
    lax.fori_loop(0, cols // 2, first, 0)
    for i in range(2):
        edges_of(held.at[0, i], edges.at[0], i)

    pl.semaphore_wait(barrier, expected)
    all_sends(0, lambda copy: copy.start())
    for stage in range(2):
        cache_sends(stage, lambda copy: copy.start())
    conv(0)

    def second(j, _):
        for i in range(2):
            v = acc[i, pl.ds(j * 32, 32)]
            held[1, i, pl.ds(2 * j, 2)] = silu(normed_by(v, gain2[...])).astype(BF16).reshape(2, rows, C)
        return 0
    lax.fori_loop(0, cols // 2, second, 0)
    for i in range(2):
        edges_of(held.at[1, i], edges.at[1], i)
    all_sends(1, lambda copy: copy.start())
    conv(1)

    def last(j, _):
        for i in range(2):
            v = acc[i, pl.ds(j * 32, 32)] + tok[i, pl.ds(2 * j, 2)].astype(F32).reshape(32, C)
            v = v.astype(BF16)
            stream_out[i, pl.ds(j * 32, 32)] = v
            normed_out[i, pl.ds(j * 32, 32)] = normed_by(v.astype(F32), gain_a[...]).astype(BF16)
        return 0
    lax.fori_loop(0, cols // 2, last, 0)

    for stage in range(2):
        all_sends(stage, lambda copy: copy.wait_send())
        cache_sends(stage, lambda copy: copy.wait_send())


def convs(tok, cache1, cache2, gain1, gain2, gain_a, w1, w2):
    cols, rows = tok.shape[1], tok.shape[2]
    vmem = pl.BlockSpec(memory_space=pltpu.VMEM)
    hbm = pl.BlockSpec(memory_space=pl.ANY)
    out = jax.ShapeDtypeStruct((2, cols * rows, C), BF16)
    return pl.pallas_call(
        conv_kernel,
        out_shape=(out, out),
        in_specs=[vmem] * 6 + [hbm] * 2,
        out_specs=(vmem, vmem),
        scratch_shapes=[
            pltpu.VMEM((2, 3, 3, 3, C, C), BF16),
            pltpu.VMEM((4, cols + 2, rows, 3 * C), BF16),
            pltpu.VMEM((cols + 2, 32, C), F32),
            pltpu.VMEM((2, 2, cols, rows, C), BF16),
            pltpu.VMEM((2, cols * rows, C), F32),
            pltpu.VMEM((2, 2, 2, 32, C), BF16),
            pltpu.VMEM((2, 2, 2, 32, C), BF16),
            pltpu.VMEM((2, 2, 2, 2, rows, C), BF16),
            pltpu.VMEM((2, 2, 2, 2, 32, C), BF16),
            pltpu.VMEM((2, 2, 2, 2, 2, 16, C), BF16),
            pltpu.VMEM((2, 2, cols, rows, C), BF16),
            pltpu.SemaphoreType.DMA((2, 3)),
            pltpu.SemaphoreType.DMA((2, 3, 9)),
            pltpu.SemaphoreType.DMA((2, 2, 9)),
        ],
        compiler_params=pltpu.CompilerParams(
            collective_id=0, has_side_effects=True, vmem_limit_bytes=56 << 20
        ),
    )(tok, cache1, cache2, gain1, gain2, gain_a, w1, w2)


def attn_kernel(
    normed, stream, wq, wk, wv, wo,
    out,
    blocks, query, acc, top, total, mine, back,
    send_sem, recv_sem, back_sem,
):
    tm, row, col = (lax.axis_index(a) for a in ("tm", "row", "col"))
    nrow = lax.axis_size("row")
    places = normed.shape[1]
    frame = col // 2
    other = 1 - frame
    partner = (tm, row, lax.rem(col + 2, 4))
    sibling = (tm, row, col + 1 - 2 * lax.rem(col, 2))
    up = (tm, lax.rem(row + 1, nrow), col)
    down = (tm, lax.rem(row + nrow - 1, nrow), col)

    barrier = pltpu.get_barrier_semaphore()
    for device in (partner, sibling, up, down):
        pl.semaphore_signal(barrier, inc=1, device_id=device, device_id_type=MESH)
    pl.semaphore_wait(barrier, 4)

    sent = []

    def send(src, dst, device):
        rel, half, core = dst
        copy = pltpu.make_async_remote_copy(
            src_ref=src,
            dst_ref=blocks.at[rel, half, core],
            send_sem=send_sem.at[len(sent)],
            recv_sem=recv_sem.at[rel, half, core],
            device_id=device,
            device_id_type=MESH,
        )
        copy.start()
        sent.append(copy)

    def arrived(rel, half, core):
        pltpu.make_async_remote_copy(
            src_ref=blocks.at[rel, half, core],
            dst_ref=blocks.at[rel, half, core],
            send_sem=send_sem.at[0],
            recv_sem=recv_sem.at[rel, half, core],
            device_id=partner,
            device_id_type=MESH,
        ).wait_recv()

    send(normed.at[other], (0, 1, 0), partner)
    send(normed.at[frame], (3, 0, 0), up)
    send(normed.at[frame], (1, 0, 0), down)
    send(normed.at[frame], (0, 0, 1), sibling)
    blocks[0, 0, 0] = normed[frame]

    factor = math.log2(math.e) * C ** (-0.5)

    def ask(half):
        q = jnp.dot(blocks[0, half, 0], wq[...], preferred_element_type=F32).astype(BF16)
        q = lax.dot_general(q, wk[...], (((1,), (1,)), ((), ())), preferred_element_type=F32)
        query[half] = (q * factor).astype(BF16)

    ask(0)
    top[...] = jnp.full(top.shape, -1e30, F32)
    total[...] = jnp.zeros(total.shape, F32)
    acc[...] = jnp.zeros(acc.shape, F32)

    def absorb(rel, half):
        keys = blocks[rel, half].reshape(2 * places, C)

        def step(n, _):
            for h in range(2):
                at = pl.ds(n * 128, 128)
                s = lax.dot_general(query[h, at], keys, (((1,), (1,)), ((), ())), preferred_element_type=F32)
                before = top[h, at]
                now = jnp.maximum(before, jnp.max(s, axis=-1, keepdims=True))
                shrink = jnp.exp2(before - now)
                expo = jnp.exp2(s - now[:, 0:1])
                total[h, at] = total[h, at] * shrink + jnp.sum(expo, axis=-1, keepdims=True)
                mixed = jnp.dot(expo.astype(BF16), keys, preferred_element_type=F32)
                acc[h, at] = acc[h, at] * shrink[:, 0:1] + mixed
                top[h, at] = now
            return 0
        lax.fori_loop(0, places // 128, step, 0)

    arrived(0, 1, 0)
    send(blocks.at[0, 1, 0], (3, 1, 0), up)
    send(blocks.at[0, 1, 0], (1, 1, 0), down)
    send(blocks.at[0, 1, 0], (0, 1, 1), sibling)
    ask(1)
    arrived(3, 0, 0)
    send(blocks.at[3, 0, 0], (2, 0, 0), up)
    send(blocks.at[3, 0, 0], (3, 0, 1), sibling)
    arrived(1, 0, 0)
    send(blocks.at[1, 0, 0], (1, 0, 1), sibling)
    arrived(0, 0, 1)
    absorb(0, 0)
    arrived(0, 1, 1)
    absorb(0, 1)
    arrived(3, 1, 0)
    send(blocks.at[3, 1, 0], (3, 1, 1), sibling)
    arrived(1, 1, 0)
    send(blocks.at[1, 1, 0], (2, 1, 0), down)
    send(blocks.at[1, 1, 0], (1, 1, 1), sibling)
    arrived(3, 0, 1)
    absorb(3, 0)
    arrived(1, 0, 1)
    absorb(1, 0)
    arrived(2, 0, 0)
    send(blocks.at[2, 0, 0], (2, 0, 1), sibling)
    arrived(3, 1, 1)
    absorb(3, 1)
    arrived(2, 1, 0)
    send(blocks.at[2, 1, 0], (2, 1, 1), sibling)
    arrived(1, 1, 1)
    absorb(1, 1)
    arrived(2, 0, 1)
    absorb(2, 0)
    arrived(2, 1, 1)
    absorb(2, 1)

    def attended(h):
        mixed = (acc[h] / total[h][:, 0:1]).astype(BF16)
        return jnp.dot(mixed, wv[...], preferred_element_type=F32).astype(BF16)

    def finish(at, values):
        out[at] = (stream[at].astype(F32) + jnp.dot(values, wo[...], preferred_element_type=F32)).astype(BF16)

    mine[...] = attended(1)
    copy = pltpu.make_async_remote_copy(
        src_ref=mine, dst_ref=back, send_sem=back_sem.at[0], recv_sem=back_sem.at[1],
        device_id=partner, device_id_type=MESH,
    )
    copy.start()
    finish(frame, attended(0))
    copy.wait()
    finish(other, back[...])
    for copy in sent:
        copy.wait_send()


def attention(normed, stream, wq, wk, wv, wo):
    places = normed.shape[1]
    vmem = pl.BlockSpec(memory_space=pltpu.VMEM)
    return pl.pallas_call(
        attn_kernel,
        out_shape=jax.ShapeDtypeStruct(normed.shape, BF16),
        in_specs=[vmem] * 6,
        out_specs=vmem,
        scratch_shapes=[
            pltpu.VMEM((4, 2, 2, places, C), BF16),
            pltpu.VMEM((2, places, C), BF16),
            pltpu.VMEM((2, places, C), F32),
            pltpu.VMEM((2, places, 128), F32),
            pltpu.VMEM((2, places, 128), F32),
            pltpu.VMEM((places, C), BF16),
            pltpu.VMEM((places, C), BF16),
            pltpu.SemaphoreType.DMA((20,)),
            pltpu.SemaphoreType.DMA((4, 2, 2)),
            pltpu.SemaphoreType.DMA((2,)),
        ],
        compiler_params=pltpu.CompilerParams(
            collective_id=1, has_side_effects=True, vmem_limit_bytes=48 << 20
        ),
    )(normed, stream, wq, wk, wv, wo)


def on_device(
    tokens, cache_first, cache_second, gain_first, gain_second, conv_first, conv_second,
    gain_attn, query_weight, key_weight, value_weight, out_weight,
):
    count, rows, cols, chans = tokens.shape
    swap = lambda v: jnp.swapaxes(v, 1, 2)
    stream, normed = convs(
        swap(tokens), swap(cache_first), swap(cache_second),
        gain_first[None], gain_second[None], gain_attn[None], conv_first, conv_second,
    )
    out = attention(normed, stream, query_weight, key_weight, value_weight, out_weight)
    return swap(out.reshape(count, cols, rows, chans))


def solution(mesh):
    spread, kept = P("tm", "row", "col", None), P(None, "row", "col", None)
    return jax.shard_map(
        on_device,
        mesh=mesh,
        in_specs=(spread, kept, kept) + (P(),) * 9,
        out_specs=spread,
        check_vma=False,
    )
```

```python
import math

import jax
import jax.numpy as jnp
from jax import lax
from jax.experimental import pallas as pl
from jax.experimental.pallas import tpu as pltpu
from jax.sharding import PartitionSpec as P

MESH = pl.DeviceIdType.MESH
F32 = jnp.float32
BF16 = jnp.bfloat16
C, ROWS, COLS = 384, 16, 24
PLACES = ROWS * COLS
SIDES = [(dr, dc) for dr in (-1, 0, 1) for dc in (-1, 0, 1) if (dr, dc) != (0, 0)]
INNER = {8: -1, 9: 1}
SENT = {0: (((0, 9), (15, 24)), ((9, 15),)), 1: (((0, 8), (16, 24)), ((8, 16),))}
DONE = {0: (((0, 8), (16, 24)), ((8, 16),)), 1: (((0, 7), (17, 24)), ((7, 17),))}
BUILT = {0: (((0, 10), (16, 26)), ((10, 16),)), 1: (((0, 9), (17, 26)), ((9, 17),))}
PIECES = ((0, 224), (224, 160))
LIFTED = 32
LANES = C // 128


def normed_by(v, gain):
    return v * lax.rsqrt(jnp.mean(v * v, axis=-1, keepdims=True) + 1e-06) * gain


def each(lo, hi, body, unroll):
    def step(n, _):
        body(n)
        return 0
    lax.fori_loop(lo, hi, step, 0, unroll=min(unroll, hi - lo))


def silu(v):
    return v / (1.0 + jnp.exp(-v))


def kernel(
    tok, cache1, cache2, gain1, gain2, gain_a, w1, w2, wq, wk, wv, wo,
    out,
    wbuf, views, lift, tok_t, held, acc, cache_in,
    edge_o, edge_i, corner, cache_o, cache_i, cache_k,
    halo_c, halo_o, halo_i, halo_k, halo_t,
    normed, stream, blocks, query, mixed, top, total, mine, back,
    w_sem, cache_sem, send_sem, recv_sem, attn_send, attn_recv, back_sem,
):
    ntm, nrow, ncol = (lax.axis_size(a) for a in ("tm", "row", "col"))
    tm, row, col = (lax.axis_index(a) for a in ("tm", "row", "col"))
    partner = (tm, row, lax.rem(col + 2, ncol))
    sibling = (tm, row, col + 1 - 2 * lax.rem(col, 2))
    up = (tm, lax.rem(row + 1, nrow), col)
    down = (tm, lax.rem(row + nrow - 1, nrow), col)
    lines = lift.reshape(LANES, (COLS + 2) * LIFTED, 128)

    def put_line(at, first, v):
        for k in range(LANES):
            lines[k, pl.ds(first * LIFTED + 8 + at, v.shape[0], stride=LIFTED), :] = v[:, k * 128:(k + 1) * 128]

    def get_line(at, first, count):
        return jnp.concatenate([
            lines[k, pl.ds(first * LIFTED + 8 + at, count, stride=LIFTED), :] for k in range(LANES)
        ], axis=1)

    def put_column(j, at, v):
        for k in range(LANES):
            lift[k, j, 8 + at:8 + at + v.shape[0], :] = v[:, k * 128:(k + 1) * 128]

    def get_column(j, at, count):
        return jnp.concatenate([lift[k, j, 8 + at:8 + at + count, :] for k in range(LANES)], axis=1)

    def there(dr, dc):
        ok = (row + dr >= 0) & (row + dr < nrow)
        return ok & (col + dc >= 0) & (col + dc < ncol)

    barrier = pltpu.get_barrier_semaphore()
    for dr, dc in SIDES:
        @pl.when(there(dr, dc))
        def _():
            pl.semaphore_signal(barrier, inc=1, device_id=(tm, row + dr, col + dc), device_id_type=MESH)

        @pl.when(there(dr, dc) & (tm > 0))
        def _():
            pl.semaphore_signal(barrier, inc=1, device_id=(tm - 1, row + dr, col + dc), device_id_type=MESH)

    @pl.when(tm > 0)
    def _():
        pl.semaphore_signal(barrier, inc=1, device_id=(tm - 1, row, col), device_id_type=MESH)

    for device in (partner, sibling, up, down):
        pl.semaphore_signal(barrier, inc=1, device_id=device, device_id_type=MESH)

    def as_int(flag):
        return jnp.where(flag, 1, 0)

    around = (1 + as_int(row > 0) + as_int(row < nrow - 1)) * (1 + as_int(col > 0) + as_int(col < ncol - 1))
    expected = around - 1 + jnp.where(tm < ntm - 1, around, 0) + 4

    caches = [
        pltpu.make_async_copy(src, cache_in.at[stage], cache_sem.at[stage])
        for stage, src in ((0, cache1), (1, cache2))
    ]

    @pl.when(tm == 0)
    def _():
        for copy in caches:
            copy.start()

    weights = []
    for stage, src in ((0, w1), (1, w2)):
        for a in (2, 1, 0):
            for c in range(3):
                copy = pltpu.make_async_copy(
                    src.at[a, :, c],
                    wbuf.at[stage, c, :, :, pl.ds((2 - a) * C, C)],
                    w_sem.at[stage, a],
                )
                copy.start()
                weights.append((stage, a, copy))

    def wait_weights(stage, a):
        for s, b, copy in weights:
            if (s, b) == (stage, a):
                copy.wait()

    def step_of(k):
        return (INNER[k], 0) if k in INNER else SIDES[k]

    def side_copy(stage, group, k):
        dr, dc = step_of(k)
        pair = 1 if group == 0 else 0
        tile = halo_t if group == 2 else held
        e_o, e_i, e_k = (cache_o, cache_i, cache_k) if group == 2 else (edge_o, edge_i, corner)
        line, top_at = (1, 0) if dr == 1 else (0, 1)
        lr = 0 if dc == 1 else 1
        if k in INNER:
            src, dst = e_i.at[stage, line], halo_i.at[stage, pair, top_at]
        elif dr == 0:
            src, dst = tile.at[stage, :, COLS - 1 if dc == 1 else 0], halo_c.at[stage, pair, :, lr]
        elif dc == 0:
            src, dst = e_o.at[stage, line], halo_o.at[stage, pair, top_at]
        else:
            src, dst = e_k.at[stage], halo_k.at[stage, pair, top_at, lr]
        return pltpu.make_async_remote_copy(
            src_ref=src,
            dst_ref=dst,
            send_sem=send_sem.at[stage, group, k],
            recv_sem=recv_sem.at[stage, pair, k],
            device_id=(tm + 1 if group == 1 else tm, row + dr, col + dc),
            device_id_type=MESH,
        )

    def tile_copies(stage, part):
        made = []
        for n, (lo, hi) in enumerate(SENT[stage][part]):
            k = 10 + 2 * part + n
            made.append(pltpu.make_async_remote_copy(
                src_ref=held.at[stage, :, pl.ds(lo, hi - lo)],
                dst_ref=halo_t.at[stage, :, pl.ds(lo, hi - lo)],
                send_sem=send_sem.at[stage, 1, k],
                recv_sem=recv_sem.at[stage, 0, k],
                device_id=(tm + 1, row, col),
                device_id_type=MESH,
            ))
        return made

    def sides_in(part):
        return tuple(INNER) if part else tuple(range(8))

    def side_sends(stage, group, part, act):
        for k in sides_in(part):
            ok = there(*step_of(k))
            if group == 1:
                ok = ok & (tm < ntm - 1)
            if group == 2:
                ok = ok & (tm == 0)

            @pl.when(ok)
            def _():
                act(side_copy(stage, group, k))

    def tile_sends(stage, part, act):
        @pl.when(tm < ntm - 1)
        def _():
            for copy in tile_copies(stage, part):
                act(copy)

    def start(copy):
        copy.start()

    def wait_sides(stage, pair, part):
        for k in sides_in(part):
            dr, dc = step_of(k)

            @pl.when(there(-dr, -dc))
            def _():
                side_copy(stage, 1 - pair, k).wait_recv()

    def wait_tile(stage, part):
        @pl.when(tm > 0)
        def _():
            for copy in tile_copies(stage, part):
                copy.wait_recv()

    def take_lines(stage, i, part, e_o, e_k):
        for line, at in ((0, 0), (1, ROWS - 1)):
            if part == 0:
                both = [get_line(at, 1, 8), get_line(at, 17, 8)]
                e_o[stage, line, i] = jnp.concatenate(both, axis=0).astype(BF16)
        if part == 0:
            fill = jnp.zeros((2, C), F32)
            rows = []
            for at in (0, ROWS - 1):
                rows += [get_column(1, at, 1), get_column(COLS, at, 1), fill]
            return jnp.concatenate(rows, axis=0)

    def inner_lines():
        return [get_line(at, 9, 8) for at in (0, ROWS - 1)]

    def lift_columns(src, lo, hi):
        def step(j):
            put_column(j + 1, 0, src[j].astype(F32))
        each(lo, hi, step, 4)

    def lift_lines(stage, pair, i, part):
        for t, at in ((0, -1), (1, ROWS)):
            if part == 0:
                v = halo_o[stage, pair, t, i].astype(F32)
                put_line(at, 1, v[0:8])
                put_line(at, 17, v[8:16])
                for lr, j in ((0, 0), (1, COLS + 1)):
                    n = i * 8 + (1 - t) * 4 + (1 - lr)
                    put_column(j, at, halo_k[stage, pair, t, lr].astype(F32)[n:n + 1])
            else:
                put_line(at, 9, halo_i[stage, pair, t].astype(F32)[8 * i:8 * i + 8])
        if part == 0:
            put_column(0, 0, halo_c[stage, pair, i, 0].astype(F32))
            put_column(COLS + 1, 0, halo_c[stage, pair, i, 1].astype(F32))

    def build(slot, spans):
        def step(j):
            for b in range(3):
                views[slot, j, :, b * C:(b + 1) * C] = get_column(j, b - 1, ROWS).astype(BF16)
        for lo, hi in spans:
            each(lo, hi, step, 4)

    def window(slot, spans):
        return jnp.concatenate([
            jnp.concatenate(
                [views[slot, lo + c:hi + c].reshape((hi - lo) * ROWS, 3 * C) for c in range(3)], axis=1
            )
            for lo, hi in spans
        ], axis=0)

    def times(left, stage, lo, hi):
        right = wbuf[stage, :, :, :, lo:hi].reshape(9 * C, hi - lo)
        return jnp.dot(left, right, preferred_element_type=F32)

    def conv_own(stage):
        wait_sides(stage, 1, 0)
        wait_sides(stage, 1, 1)
        for i in range(2):
            lift_columns(held.at[stage, i], 0, COLS)
            lift_lines(stage, 1, i, 0)
            lift_lines(stage, 1, i, 1)
            build(2 + i, ((0, COLS + 2),))
        wait_weights(stage, 2)
        wait_weights(stage, 1)
        whole = ((0, COLS),)
        acc[...] = times(window(2, whole), stage, 0, 2 * C)
        acc[:, C:] += times(window(3, whole), stage, 0, C)

    def conv_before(stage, part):
        if stage == 0 and part == 0:
            wait_sides(0, 0, 1)
        if stage == 1 and part == 1:
            wait_sides(1, 0, 1)
        if part == 0:
            wait_sides(stage, 0, 0)
        wait_tile(stage, part)
        for i in range(2):
            for lo, hi in SENT[stage][part]:
                lift_columns(halo_t.at[stage, i], lo, hi)
            if part == 0:
                lift_lines(stage, 0, i, 0)
            if part == 1 or stage == 0:
                lift_lines(stage, 0, i, 1)
            build(i, BUILT[stage][part])
        if part == 0:
            wait_weights(stage, 0)
        spans = DONE[stage][part]
        near = times(window(1, spans), stage, C, 3 * C)
        far = times(window(0, spans), stage, 2 * C, 3 * C)
        n = 0
        for lo, hi in spans:
            size = (hi - lo) * ROWS
            at = slice(lo * ROWS, hi * ROWS)
            acc[at, 0:C] += near[n:n + size, 0:C] + far[n:n + size]
            acc[at, C:] += near[n:n + size, C:]
            n += size

    for k in range(10):
        dr, dc = step_of(k)
        line_at = 0 if dr == 1 else 1
        lr = 0 if dc == 1 else 1

        @pl.when(jnp.logical_not(there(-dr, -dc)))
        def _():
            for stage in range(2):
                for pair in range(2):
                    if k in INNER:
                        ref = halo_i.at[stage, pair, line_at]
                    elif dr == 0:
                        ref = halo_c.at[stage, pair, :, lr]
                    elif dc == 0:
                        ref = halo_o.at[stage, pair, line_at]
                    else:
                        ref = halo_k.at[stage, pair, line_at, lr]
                    ref[...] = jnp.zeros(ref.shape, BF16)

    corners, inners = [], []
    for i in range(2):
        def first(r):
            v = normed_by(tok[i, r].astype(F32), gain1[...])
            put_line(r, 1, silu(v).astype(BF16).astype(F32))
        each(0, ROWS, first, 8)

        def settle(j):
            held[0, i, j] = get_column(j + 1, 0, ROWS).astype(BF16)
        each(0, COLS, settle, 8)
        corners.append(take_lines(0, i, 0, edge_o, corner))
        inners.append(inner_lines())
    corner[0] = jnp.concatenate(corners, axis=0).astype(BF16)
    for line in range(2):
        edge_i[0, line] = jnp.concatenate([inners[0][line], inners[1][line]], axis=0).astype(BF16)

    pl.semaphore_wait(barrier, expected)
    for part in range(2):
        side_sends(0, 0, part, start)
    for part in range(2):
        side_sends(0, 1, part, start)
    for part in range(2):
        tile_sends(0, part, start)

    @pl.when(tm == 0)
    def _():
        for stage in range(2):
            caches[stage].wait()
            corners, inners = [], []
            for i in range(2):
                def turn(r):
                    put_line(r, 1, cache_in[stage, i, r].astype(F32))
                each(0, ROWS, turn, 8)

                def settle(j):
                    halo_t[stage, i, j] = get_column(j + 1, 0, ROWS).astype(BF16)
                each(0, COLS, settle, 8)
                corners.append(take_lines(stage, i, 0, cache_o, cache_k))
                inners.append(inner_lines())
            cache_k[stage] = jnp.concatenate(corners, axis=0).astype(BF16)
            for line in range(2):
                cache_i[stage, line] = jnp.concatenate(
                    [inners[0][line], inners[1][line]], axis=0
                ).astype(BF16)
    for stage in range(2):
        for part in range(2):
            side_sends(stage, 2, part, start)

    for i in range(2):
        def turn(r):
            put_line(r, 1, tok[i, r].astype(F32))
        each(0, ROWS, turn, 8)

        def settle(j):
            tok_t[i, j] = get_column(j + 1, 0, ROWS).astype(BF16)
        each(0, COLS, settle, 8)

    conv_own(0)
    for part in range(2):
        conv_before(0, part)
        corners, inners = [], []
        for i in range(2):
            def second(j):
                v = normed_by(acc[pl.ds(j * ROWS, ROWS), i * C:(i + 1) * C], gain2[...])
                v = silu(v).astype(BF16)
                held[1, i, j] = v
                put_column(j + 1, 0, v.astype(F32))
            for lo, hi in DONE[0][part]:
                each(lo, hi, second, 8)
            if part == 0:
                corners.append(take_lines(1, i, 0, edge_o, corner))
            else:
                inners.append(inner_lines())
        if part == 0:
            corner[1] = jnp.concatenate(corners, axis=0).astype(BF16)
        else:
            for line in range(2):
                edge_i[1, line] = jnp.concatenate([inners[0][line], inners[1][line]], axis=0).astype(BF16)
        side_sends(1, 0, part, start)
        side_sends(1, 1, part, start)
        tile_sends(1, part, start)

    frame = col // 2
    other = 1 - frame
    sent = []

    def send(src, dst, piece, device):
        rel, half, core = dst
        lo, size = PIECES[piece]
        copy = pltpu.make_async_remote_copy(
            src_ref=src.at[pl.ds(lo, size)],
            dst_ref=blocks.at[rel, half, core, pl.ds(lo, size)],
            send_sem=attn_send.at[len(sent)],
            recv_sem=attn_recv.at[rel, half, core, piece],
            device_id=device,
            device_id_type=MESH,
        )
        copy.start()
        sent.append(copy)

    def arrived(rel, half, core, piece):
        lo, size = PIECES[piece]
        ref = blocks.at[rel, half, core, pl.ds(lo, size)]
        pltpu.make_async_remote_copy(
            src_ref=ref, dst_ref=ref,
            send_sem=attn_send.at[0], recv_sem=attn_recv.at[rel, half, core, piece],
            device_id=partner, device_id_type=MESH,
        ).wait_recv()

    conv_own(1)
    for part in range(2):
        conv_before(1, part)
        n = PIECES[part][0]
        for lo, hi in DONE[1][part]:
            for i in range(2):
                def last(j):
                    at = pl.ds(pl.multiple_of(n + (j - lo) * ROWS, ROWS), ROWS)
                    v = acc[pl.ds(pl.multiple_of(j * ROWS, ROWS), ROWS), i * C:(i + 1) * C]
                    v = (v + tok_t[i, j].astype(F32)).astype(BF16)
                    stream[i, at] = v
                    normed[i, at] = normed_by(v.astype(F32), gain_a[...]).astype(BF16)
                each(lo, hi, last, 8)
            n += (hi - lo) * ROWS
        send(normed.at[other], (0, 1, 0), part, partner)
        send(normed.at[frame], (3, 0, 0), part, up)
        send(normed.at[frame], (1, 0, 0), part, down)
        send(normed.at[frame], (0, 0, 1), part, sibling)

    blocks[0, 0, 0] = normed[frame]
    factor = math.log2(math.e) * C ** (-0.5)

    def ask(half):
        q = jnp.dot(blocks[0, half, 0], wq[...], preferred_element_type=F32).astype(BF16)
        q = lax.dot_general(wk[...], q, (((1,), (1,)), ((), ())), preferred_element_type=F32)
        query[:, half * PLACES:(half + 1) * PLACES] = (q * factor).astype(BF16)

    def absorb(rel, half, initial=False):
        keys = blocks[rel, half].reshape(2 * PLACES, C)
        s = jnp.dot(keys, query[...], preferred_element_type=F32)
        now = jnp.max(s, axis=0, keepdims=True)
        if not initial:
            before = top[0:1]
            now = jnp.maximum(before, now)
            shrink = jnp.exp2(before - now)
        expo = jnp.exp2(s - now)
        summed = jnp.sum(expo, axis=0, keepdims=True)
        new = lax.dot_general(
            keys, expo.astype(BF16), (((0,), (0,)), ((), ())), preferred_element_type=F32
        )
        if initial:
            total[0:1] = summed
            mixed[...] = new
        else:
            total[0:1] = total[0:1] * shrink + summed
            mixed[...] = mixed[...] * shrink + new
        top[0:1] = now

    def relay(src, moves):
        for piece in range(2):
            arrived(*src, piece)
            for dst, device in moves:
                send(blocks.at[src], dst, piece, device)

    def ready(rel, half):
        for piece in range(2):
            arrived(rel, half, 1, piece)

    ask(0)
    relay((0, 1, 0), (((3, 1, 0), up), ((1, 1, 0), down), ((0, 1, 1), sibling)))
    ask(1)
    relay((3, 0, 0), (((2, 0, 0), up), ((3, 0, 1), sibling)))
    relay((1, 0, 0), (((1, 0, 1), sibling),))
    ready(0, 0)
    absorb(0, 0, True)
    ready(0, 1)
    absorb(0, 1)
    relay((3, 1, 0), (((3, 1, 1), sibling),))
    relay((1, 1, 0), (((2, 1, 0), down), ((1, 1, 1), sibling)))
    ready(3, 0)
    absorb(3, 0)
    ready(1, 0)
    absorb(1, 0)
    relay((2, 0, 0), (((2, 0, 1), sibling),))
    ready(3, 1)
    absorb(3, 1)
    relay((2, 1, 0), (((2, 1, 1), sibling),))
    ready(1, 1)
    absorb(1, 1)
    ready(2, 0)
    absorb(2, 0)
    ready(2, 1)
    absorb(2, 1)

    def attended(h):
        at = slice(h * PLACES, (h + 1) * PLACES)
        v = (mixed[:, at] / total[0:1, at]).T.astype(BF16)
        return jnp.dot(v, wv[...], preferred_element_type=F32).astype(BF16)

    def finish(i, values):
        acc[:, 0:C] = stream[i].astype(F32) + jnp.dot(values, wo[...], preferred_element_type=F32)
        n = 0
        for part in range(2):
            for lo, hi in DONE[1][part]:
                def put(j):
                    put_column(j + 1, 0, acc[pl.ds(pl.multiple_of(n + (j - lo) * ROWS, ROWS), ROWS), 0:C])
                each(lo, hi, put, 8)
                n += (hi - lo) * ROWS

        def turn(r):
            out[i, r] = get_line(r, 1, COLS).astype(BF16)
        each(0, ROWS, turn, 8)

    mine[...] = attended(1)
    copy = pltpu.make_async_remote_copy(
        src_ref=mine, dst_ref=back, send_sem=back_sem.at[0], recv_sem=back_sem.at[1],
        device_id=partner, device_id_type=MESH,
    )
    copy.start()
    finish(frame, attended(0))
    copy.wait()
    finish(other, back[...])

    for copy in sent:
        copy.wait_send()
    for stage in range(2):
        for part in range(2):
            for group in range(3):
                side_sends(stage, group, part, lambda copy: copy.wait_send())
            tile_sends(stage, part, lambda copy: copy.wait_send())


def on_device(
    tokens, cache_first, cache_second, gain_first, gain_second, conv_first, conv_second,
    gain_attn, query_weight, key_weight, value_weight, out_weight,
):
    vmem = pl.BlockSpec(memory_space=pltpu.VMEM)
    hbm = pl.BlockSpec(memory_space=pl.ANY)
    return pl.pallas_call(
        kernel,
        out_shape=jax.ShapeDtypeStruct(tokens.shape, BF16),
        in_specs=[vmem, hbm, hbm, vmem, vmem, vmem, hbm, hbm, vmem, vmem, vmem, vmem],
        out_specs=vmem,
        scratch_shapes=[
            pltpu.VMEM((2, 3, 3, C, 3 * C), BF16),
            pltpu.VMEM((4, COLS + 2, ROWS, 3 * C), BF16),
            pltpu.VMEM((LANES, COLS + 2, LIFTED, 128), F32),
            pltpu.VMEM((2, COLS, ROWS, C), BF16),
            pltpu.VMEM((2, 2, COLS, ROWS, C), BF16),
            pltpu.VMEM((PLACES, 2 * C), F32),
            pltpu.VMEM((2, 2, ROWS, COLS, C), BF16),
            pltpu.VMEM((2, 2, 2, 16, C), BF16),
            pltpu.VMEM((2, 2, 16, C), BF16),
            pltpu.VMEM((2, 16, C), BF16),
            pltpu.VMEM((2, 2, 2, 16, C), BF16),
            pltpu.VMEM((2, 2, 16, C), BF16),
            pltpu.VMEM((2, 16, C), BF16),
            pltpu.VMEM((2, 2, 2, 2, 16, C), BF16),
            pltpu.VMEM((2, 2, 2, 2, 16, C), BF16),
            pltpu.VMEM((2, 2, 2, 16, C), BF16),
            pltpu.VMEM((2, 2, 2, 2, 16, C), BF16),
            pltpu.VMEM((2, 2, COLS, ROWS, C), BF16),
            pltpu.VMEM((2, PLACES, C), BF16),
            pltpu.VMEM((2, PLACES, C), BF16),
            pltpu.VMEM((4, 2, 2, PLACES, C), BF16),
            pltpu.VMEM((C, 2 * PLACES), BF16),
            pltpu.VMEM((C, 2 * PLACES), F32),
            pltpu.VMEM((8, 2 * PLACES), F32),
            pltpu.VMEM((8, 2 * PLACES), F32),
            pltpu.VMEM((PLACES, C), BF16),
            pltpu.VMEM((PLACES, C), BF16),
            pltpu.SemaphoreType.DMA((2, 3)),
            pltpu.SemaphoreType.DMA((2,)),
            pltpu.SemaphoreType.DMA((2, 3, 14)),
            pltpu.SemaphoreType.DMA((2, 2, 14)),
            pltpu.SemaphoreType.DMA((40,)),
            pltpu.SemaphoreType.DMA((4, 2, 2, 2)),
            pltpu.SemaphoreType.DMA((2,)),
        ],
        compiler_params=pltpu.CompilerParams(
            collective_id=0, has_side_effects=True, vmem_limit_bytes=58 << 20
        ),
    )(
        tokens, cache_first, cache_second, gain_first, gain_second, gain_attn, conv_first, conv_second,
        query_weight, key_weight, value_weight, out_weight,
    )


def solution(mesh):
    spread, kept = P("tm", "row", "col", None), P(None, "row", "col", None)
    return jax.shard_map(
        on_device,
        mesh=mesh,
        in_specs=(spread, kept, kept) + (P(),) * 9,
        out_specs=spread,
        check_vma=False,
    )
```

```python
import math

import jax
import jax.numpy as jnp
from jax import lax
from jax.experimental import pallas as pl
from jax.experimental.pallas import tpu as pltpu
from jax.sharding import PartitionSpec as P

MESH = pl.DeviceIdType.MESH
F32 = jnp.float32
BF16 = jnp.bfloat16
C, ROWS, COLS = 384, 16, 24
RING = 4
STRIP = COLS // RING
WIDE = STRIP + 2
CUT = STRIP * ROWS
PLACES = ROWS * COLS
PIECES = ((0, CUT), (CUT, CUT), (2 * CUT, 2 * CUT))
LIFTED = 32
LANES = C // 128


def normed_by(v, gain):
    return v * lax.rsqrt(jnp.mean(v * v, axis=-1, keepdims=True) + 1e-06) * gain


def each(lo, hi, body, unroll):
    def step(n, _):
        body(n)
        return 0
    lax.fori_loop(lo, hi, step, 0, unroll=min(unroll, hi - lo))


def silu(v):
    return v / (1.0 + jnp.exp(-v))


def kernel(
    tok, cache1, cache2, gain1, gain2, gain_a, w1, w2, wq, wk, wv, wo,
    out,
    wbuf, views, lift, tok_t, raw, padded, lines_out, lines_in, corners_in, cache_in, made, final,
    normed, stream, blocks, query, mixed, top, total, mine, back,
    w_sem, cache_sem, ring_send, ring_recv, halo_send, halo_recv,
    past_send, past_recv, home_send, home_recv, attn_send, attn_recv, back_sem,
):
    nrow, ncol = lax.axis_size("row"), lax.axis_size("col")
    tm, row, col = (lax.axis_index(a) for a in ("tm", "row", "col"))
    x = lax.rem(tm, RING)
    ring = tm - x
    early = tm < RING
    strip = col * RING + x
    left_ok, right_ok = strip > 0, strip < ncol * RING - 1
    left = (jnp.where(x > 0, tm - 1, tm + RING - 1), row, jnp.where(x > 0, col, col - 1))
    right = (jnp.where(x < RING - 1, tm + 1, tm - RING + 1), row, jnp.where(x < RING - 1, col, col + 1))
    partner = (tm, row, lax.rem(col + 2, ncol))
    sibling = (tm, row, col + 1 - 2 * lax.rem(col, 2))
    up = (tm, lax.rem(row + 1, nrow), col)
    down = (tm, lax.rem(row + nrow - 1, nrow), col)

    def around(step):
        return lax.rem(x + step + RING, RING)

    @pl.when(jnp.logical_not(left_ok))
    def _():
        padded[:, :, 0] = jnp.zeros((2, 2 * RING + 2, ROWS, C), BF16)
        corners_in[:, :, :, 0] = jnp.zeros((2, RING + 1, 2, 16, C), BF16)

    @pl.when(jnp.logical_not(right_ok))
    def _():
        padded[:, :, WIDE - 1] = jnp.zeros((2, 2 * RING + 2, ROWS, C), BF16)
        corners_in[:, :, :, 1] = jnp.zeros((2, RING + 1, 2, 16, C), BF16)

    @pl.when(row == 0)
    def _():
        lines_in[:, :, 0] = jnp.zeros((2, RING + 1, 16, C), BF16)
        corners_in[:, :, 0] = jnp.zeros((2, RING + 1, 2, 16, C), BF16)

    @pl.when(row == nrow - 1)
    def _():
        lines_in[:, :, 1] = jnp.zeros((2, RING + 1, 16, C), BF16)
        corners_in[:, :, 1] = jnp.zeros((2, RING + 1, 2, 16, C), BF16)

    barrier = pltpu.get_barrier_semaphore()

    def greet(device):
        pl.semaphore_signal(barrier, inc=1, device_id=device, device_id_type=MESH)

    for step in range(1, RING):
        greet((ring + around(step), row, col))
    for device in (partner, sibling, up, down):
        greet(device)

    @pl.when(left_ok)
    def _():
        greet(left)

    @pl.when(right_ok)
    def _():
        greet(right)

    for ok, side in ((left_ok, left), (right_ok, right)):
        @pl.when(ok & (row > 0))
        def _():
            greet((side[0], row - 1, side[2]))

        @pl.when(ok & (row < nrow - 1))
        def _():
            greet((side[0], row + 1, side[2]))

    @pl.when(jnp.logical_not(early))
    def _():
        greet((tm - RING, row, col))

    def as_int(flag):
        return jnp.where(flag, 1, 0)

    beside = as_int(left_ok) + as_int(right_ok)
    above = as_int(row > 0) + as_int(row < nrow - 1)
    expected = RING - 1 + 4 + beside * (1 + above) + as_int(early)

    caches = [
        pltpu.make_async_copy(src, cache_in.at[stage], cache_sem.at[stage])
        for stage, src in ((0, cache1), (1, cache2))
    ]

    @pl.when(early)
    def _():
        for copy in caches:
            copy.start()

    weights = []
    for stage, src in ((0, w1), (1, w2)):
        for a in range(3):
            for c in range(3):
                copy = pltpu.make_async_copy(src.at[a, :, c], wbuf.at[stage, a, c], w_sem.at[stage])
                copy.start()
                weights.append((stage, copy))

    def wait_weights(stage):
        for s, copy in weights:
            if s == stage:
                copy.wait()

    lines = lift.reshape(LANES, COLS * LIFTED, 128)

    def put_line(at, v):
        for k in range(LANES):
            lines[k, pl.ds(8 + at, v.shape[0], stride=LIFTED), :] = v[:, k * 128:(k + 1) * 128]

    def get_line(at, count):
        return jnp.concatenate([
            lines[k, pl.ds(8 + at, count, stride=LIFTED), :] for k in range(LANES)
        ], axis=1)

    def put_column(j, v):
        for k in range(LANES):
            lift[k, j, 8:8 + ROWS, :] = v[:, k * 128:(k + 1) * 128]

    def get_column(j, at):
        return jnp.concatenate([lift[k, j, 8 + at:8 + at + ROWS, :] for k in range(LANES)], axis=1)

    def halo_copies(stage, p):
        frames = pl.ds(2 * p, 2)
        made = []

        def copy(ok, from_ok, src, dst, device):
            k = len(made)
            made.append((ok, from_ok, pltpu.make_async_remote_copy(
                src_ref=src, dst_ref=dst,
                send_sem=halo_send.at[stage, p, k], recv_sem=halo_recv.at[stage, p, k],
                device_id=device, device_id_type=MESH,
            )))

        for ok, from_ok, mine_at, theirs, device in (
            (left_ok, right_ok, 1, WIDE - 1, left), (right_ok, left_ok, WIDE - 2, 0, right)
        ):
            copy(ok, from_ok, padded.at[stage, frames, mine_at], padded.at[stage, frames, theirs], device)
        for n, (ok, from_ok, to_row) in enumerate((
            (row > 0, row < nrow - 1, row - 1), (row < nrow - 1, row > 0, row + 1)
        )):
            src = lines_out.at[stage, p, n]
            copy(ok, from_ok, src, lines_in.at[stage, p, 1 - n], (tm, to_row, col))
            copy(ok & left_ok, from_ok & right_ok, src, corners_in.at[stage, p, 1 - n, 1],
                 (left[0], to_row, left[2]))
            copy(ok & right_ok, from_ok & left_ok, src, corners_in.at[stage, p, 1 - n, 0],
                 (right[0], to_row, right[2]))
        return made

    def on(pairs, act):
        for ok, copy in pairs:
            @pl.when(ok)
            def _():
                act(copy)

    def start(copy):
        copy.start()

    def wait_recv(copy):
        copy.wait_recv()

    def wait_send(copy):
        copy.wait_send()

    def await_halo(stage, p):
        on([(from_ok, copy) for _, from_ok, copy in halo_copies(stage, p)], wait_recv)

    def send_halo(stage, p):
        def step(n):
            for i in range(2):
                put_column(WIDE * i + n, padded[stage, 2 * p + i, n].astype(F32))
        each(1, WIDE - 1, step, STRIP)
        for n, at in ((0, 0), (1, ROWS - 1)):
            lines_out[stage, p, n] = get_line(at, 2 * WIDE).astype(BF16)
        on([(ok, copy) for ok, _, copy in halo_copies(stage, p)], start)

    def build(stage, p):
        def up_step(n):
            for i in range(2):
                put_column(WIDE * i + n, padded[stage, 2 * p + i, n].astype(F32))
        each(0, WIDE, up_step, WIDE)
        for t, at in ((0, -1), (1, ROWS)):
            put_line(at, lines_in[stage, p, t].astype(F32))
            for lr, theirs, mine_at in ((0, WIDE - 2, 0), (1, 1, WIDE - 1)):
                v = corners_in[stage, p, t, lr].astype(F32)
                for i in range(2):
                    for k in range(LANES):
                        lift[k, WIDE * i + mine_at, 8 + at:9 + at, :] = (
                            v[WIDE * i + theirs:WIDE * i + theirs + 1, k * 128:(k + 1) * 128]
                        )

        def step(n):
            for i in range(2):
                for b in range(3):
                    views[2 * p + i, n, :, b * C:(b + 1) * C] = get_column(WIDE * i + n, b - 1).astype(BF16)
        each(0, WIDE, step, 4)

    def past_copies(stage):
        device = (tm + RING, row, col)
        return [
            pltpu.make_async_remote_copy(
                src_ref=src, dst_ref=dst,
                send_sem=past_send.at[stage, n], recv_sem=past_recv.at[stage, n],
                device_id=device, device_id_type=MESH,
            )
            for n, (src, dst) in enumerate((
                (padded.at[stage, pl.ds(2 * RING, 2)], padded.at[stage, pl.ds(0, 2)]),
                (lines_in.at[stage, RING], lines_in.at[stage, 0]),
                (corners_in.at[stage, RING], corners_in.at[stage, 0]),
            ))
        ]

    def send_past(stage):
        @pl.when(early)
        def _():
            for copy in past_copies(stage):
                copy.start()

    def build_past(stage):
        @pl.when(early)
        def _():
            await_halo(stage, 0)

        @pl.when(jnp.logical_not(early))
        def _():
            for copy in past_copies(stage):
                copy.wait_recv()
        build(stage, 0)

    def conv(stage, p):
        parts = [
            views[pl.ds(2 * p - 2 + a, 2), c:c + STRIP].reshape(2 * CUT, 3 * C)
            for a in range(3) for c in range(3)
        ]
        whole = jnp.concatenate(parts, axis=1)
        return jnp.dot(whole, wbuf[stage].reshape(27 * C, C), preferred_element_type=F32)

    for i in range(2):
        def turn(r):
            put_line(r, tok[i, r].astype(F32))
        each(0, ROWS, turn, 8)

        def settle(j):
            tok_t[i, j] = get_column(j, 0).astype(BF16)
        each(0, COLS, settle, 8)

    def ring_copy(step):
        return pltpu.make_async_remote_copy(
            src_ref=tok_t.at[:, pl.ds(STRIP * around(step), STRIP)],
            dst_ref=raw.at[pl.ds(2 * x, 2)],
            send_sem=ring_send.at[step - 1],
            recv_sem=ring_recv.at[step - 1],
            device_id=(ring + around(step), row, col),
            device_id_type=MESH,
        )

    pl.semaphore_wait(barrier, expected)
    for step in (2, 1, 3):
        ring_copy(step).start()

    @pl.when(early)
    def _():
        for stage in range(2):
            caches[stage].wait()
            for i in range(2):
                def turn(r):
                    put_line(r, cache_in[stage, i, r].astype(F32))
                each(0, ROWS, turn, 8)

                def settle(j):
                    padded[stage, i, 1 + j] = get_column(STRIP * x + j, 0).astype(BF16)
                each(0, STRIP, settle, 8)
            send_halo(stage, 0)

    def first(p):
        for i in range(2):
            def step(j):
                v = raw[2 * p - 2 + i, j].astype(F32)
                padded[0, 2 * p + i, 1 + j] = silu(normed_by(v, gain1[...])).astype(BF16)
            each(0, STRIP, step, STRIP)
        send_halo(0, p)

    raw[pl.ds(2 * x, 2)] = tok_t[:, pl.ds(STRIP * x, STRIP)]
    first(1 + x)

    for step in (1, 3, 2):
        ring_copy(step).wait_recv()
        first(1 + around(-step))
    order = tuple(range(RING, 0, -1))
    for p in order:
        await_halo(0, p)
        if p == RING:
            send_past(0)
        build(0, p)
    wait_weights(0)

    def follow(n):
        if 0 <= n < RING:
            await_halo(1, order[n])
            if order[n] == RING:
                send_past(1)
            build(1, order[n])

    for n, p in enumerate(order):
        if p == 1:
            build_past(0)
        made[...] = conv(0, p)

        def second(j):
            for i in range(2):
                v = made[pl.ds(pl.multiple_of(i * CUT + j * ROWS, ROWS), ROWS)]
                padded[1, 2 * p + i, 1 + j] = silu(normed_by(v, gain2[...])).astype(BF16)
        each(0, STRIP, second, STRIP)
        send_halo(1, p)
        follow(n - 2)
    follow(RING - 2)
    build_past(1)
    follow(RING - 1)
    wait_weights(1)

    frame = col // 2
    other = 1 - frame
    sent = []

    def send(src, dst, piece, device):
        rel, half, core = dst
        lo, size = PIECES[piece]
        copy = pltpu.make_async_remote_copy(
            src_ref=src.at[pl.ds(lo, size)],
            dst_ref=blocks.at[rel, half, core, pl.ds(lo, size)],
            send_sem=attn_send.at[len(sent)],
            recv_sem=attn_recv.at[rel, half, core, piece],
            device_id=device,
            device_id_type=MESH,
        )
        copy.start()
        sent.append(copy)

    def arrived(rel, half, core, piece):
        lo, size = PIECES[piece]
        ref = blocks.at[rel, half, core, pl.ds(lo, size)]
        pltpu.make_async_remote_copy(
            src_ref=ref, dst_ref=ref,
            send_sem=attn_send.at[0], recv_sem=attn_recv.at[rel, half, core, piece],
            device_id=partner, device_id_type=MESH,
        ).wait_recv()

    def home_copy(n):
        return pltpu.make_async_remote_copy(
            src_ref=final.at[n],
            dst_ref=stream.at[:, pl.ds(n * CUT, CUT)],
            send_sem=home_send.at[n],
            recv_sem=home_recv.at[n],
            device_id=(ring + around(n + 1), row, col),
            device_id_type=MESH,
        )

    def at_home(n):
        if n < RING - 1:
            home_copy(n).wait_recv()

        def step(j):
            for i in range(2):
                at = pl.ds(pl.multiple_of(n * CUT + j * ROWS, ROWS), ROWS)
                normed[i, at] = normed_by(stream[i, at].astype(F32), gain_a[...]).astype(BF16)
        each(0, STRIP, step, STRIP)

    def share(piece):
        send(normed.at[other], (0, 1, 0), piece, partner)
        send(normed.at[frame], (3, 0, 0), piece, up)
        send(normed.at[frame], (1, 0, 0), piece, down)
        send(normed.at[frame], (0, 0, 1), piece, sibling)

    for n in range(RING):
        p = 1 + around(n + 1)
        made[...] = conv(1, p)

        def last(j):
            for i in range(2):
                v = made[pl.ds(pl.multiple_of(i * CUT + j * ROWS, ROWS), ROWS)]
                v = (v + raw[2 * p - 2 + i, j].astype(F32)).astype(BF16)
                if n < RING - 1:
                    final[n, i, pl.ds(pl.multiple_of(j * ROWS, ROWS), ROWS)] = v
                else:
                    stream[i, pl.ds(pl.multiple_of(n * CUT + j * ROWS, ROWS), ROWS)] = v
        each(0, STRIP, last, STRIP)
        if n < RING - 1:
            home_copy(n).start()
        if n > 0:
            at_home(n - 1)
            if n < RING - 1:
                share(n - 1)
    at_home(RING - 1)
    share(2)

    blocks[0, 0, 0] = normed[frame]
    factor = math.log2(math.e) * C ** (-0.5)

    def ask(half):
        q = jnp.dot(blocks[0, half, 0], wq[...], preferred_element_type=F32).astype(BF16)
        q = lax.dot_general(wk[...], q, (((1,), (1,)), ((), ())), preferred_element_type=F32)
        query[:, half * PLACES:(half + 1) * PLACES] = (q * factor).astype(BF16)

    both, theirs = slice(0, 2 * PLACES), slice(PLACES, 2 * PLACES)

    def absorb(rel, half, at=both, initial=False):
        keys = blocks[rel, half].reshape(2 * PLACES, C)
        s = jnp.dot(keys, query[:, at], preferred_element_type=F32)
        now = jnp.max(s, axis=0, keepdims=True)
        if not initial:
            before = top[0:1, at]
            now = jnp.maximum(before, now)
            shrink = jnp.exp2(before - now)
        expo = jnp.exp2(s - now)
        summed = jnp.sum(expo, axis=0, keepdims=True)
        new = lax.dot_general(
            keys, expo.astype(BF16), (((0,), (0,)), ((), ())), preferred_element_type=F32
        )
        if initial:
            total[0:1, at] = summed
            mixed[:, at] = new
        else:
            total[0:1, at] = total[0:1, at] * shrink + summed
            mixed[:, at] = mixed[:, at] * shrink + new
        top[0:1, at] = now

    def relay(src, moves):
        for piece in range(len(PIECES)):
            arrived(*src, piece)
            for dst, device in moves:
                send(blocks.at[src], dst, piece, device)

    def ready(rel, half):
        for piece in range(len(PIECES)):
            arrived(rel, half, 1, piece)

    ask(0)
    relay((0, 1, 0), (((3, 1, 0), up), ((1, 1, 0), down), ((0, 1, 1), sibling)))
    ask(1)
    relay((3, 0, 0), (((2, 0, 0), up), ((3, 0, 1), sibling)))
    relay((1, 0, 0), (((1, 0, 1), sibling),))
    ready(0, 0)
    absorb(0, 0, both, True)
    ready(0, 1)
    absorb(0, 1)
    relay((3, 1, 0), (((3, 1, 1), sibling),))
    relay((1, 1, 0), (((2, 1, 0), down), ((1, 1, 1), sibling)))
    ready(3, 0)
    absorb(3, 0)
    ready(1, 0)
    absorb(1, 0)
    relay((2, 0, 0), (((2, 0, 1), sibling),))
    ready(3, 1)
    absorb(3, 1, theirs)
    relay((2, 1, 0), (((2, 1, 1), sibling),))
    ready(1, 1)
    absorb(1, 1, theirs)
    ready(2, 0)
    absorb(2, 0, theirs)
    ready(2, 1)
    absorb(2, 1, theirs)

    def attended(h):
        at = slice(h * PLACES, (h + 1) * PLACES)
        v = (mixed[:, at] / total[0:1, at]).T.astype(BF16)
        return jnp.dot(v, wv[...], preferred_element_type=F32).astype(BF16)

    def finish(i, values):
        v = stream[i].astype(F32) + jnp.dot(values, wo[...], preferred_element_type=F32)
        for n in range(RING):
            out[i, pl.ds(STRIP * around(-1 - n), STRIP)] = (
                v[n * CUT:(n + 1) * CUT].astype(BF16).reshape(STRIP, ROWS, C)
            )

    mine[...] = attended(1)
    copy = pltpu.make_async_remote_copy(
        src_ref=mine, dst_ref=back, send_sem=back_sem.at[0], recv_sem=back_sem.at[1],
        device_id=partner, device_id_type=MESH,
    )
    copy.start()
    for rel, half in ((3, 1), (1, 1), (2, 0), (2, 1)):
        absorb(rel, half, slice(0, PLACES))
    own = attended(0)
    finish(frame, own)
    copy.wait()
    finish(other, back[...])

    for copy in sent:
        copy.wait_send()
    for step in range(1, RING):
        ring_copy(step).wait_send()
        home_copy(step - 1).wait_send()
    for stage in range(2):
        for p in range(RING + 1):
            on([(ok & early if p == 0 else ok, copy) for ok, _, copy in halo_copies(stage, p)], wait_send)

        @pl.when(early)
        def _():
            for copy in past_copies(stage):
                copy.wait_send()


def on_device(
    tokens, cache_first, cache_second, gain_first, gain_second, conv_first, conv_second,
    gain_attn, query_weight, key_weight, value_weight, out_weight,
):
    vmem = pl.BlockSpec(memory_space=pltpu.VMEM)
    hbm = pl.BlockSpec(memory_space=pl.ANY)
    pair = (2, RING + 1, 2)
    out = pl.pallas_call(
        kernel,
        out_shape=jax.ShapeDtypeStruct((2, COLS, ROWS, C), BF16),
        in_specs=[vmem, hbm, hbm, vmem, vmem, vmem, hbm, hbm, vmem, vmem, vmem, vmem],
        out_specs=vmem,
        scratch_shapes=[
            pltpu.VMEM((2, 3, 3, 3, C, C), BF16),
            pltpu.VMEM((2 * RING + 2, WIDE, ROWS, 3 * C), BF16),
            pltpu.VMEM((LANES, COLS, LIFTED, 128), F32),
            pltpu.VMEM((2, COLS, ROWS, C), BF16),
            pltpu.VMEM((2 * RING, STRIP, ROWS, C), BF16),
            pltpu.VMEM((2, 2 * RING + 2, WIDE, ROWS, C), BF16),
            pltpu.VMEM(pair + (16, C), BF16),
            pltpu.VMEM(pair + (16, C), BF16),
            pltpu.VMEM(pair + (2, 16, C), BF16),
            pltpu.VMEM((2, 2, ROWS, COLS, C), BF16),
            pltpu.VMEM((2 * CUT, C), F32),
            pltpu.VMEM((RING - 1, 2, CUT, C), BF16),
            pltpu.VMEM((2, PLACES, C), BF16),
            pltpu.VMEM((2, PLACES, C), BF16),
            pltpu.VMEM((4, 2, 2, PLACES, C), BF16),
            pltpu.VMEM((C, 2 * PLACES), BF16),
            pltpu.VMEM((C, 2 * PLACES), F32),
            pltpu.VMEM((8, 2 * PLACES), F32),
            pltpu.VMEM((8, 2 * PLACES), F32),
            pltpu.VMEM((PLACES, C), BF16),
            pltpu.VMEM((PLACES, C), BF16),
            pltpu.SemaphoreType.DMA((2,)),
            pltpu.SemaphoreType.DMA((2,)),
            pltpu.SemaphoreType.DMA((RING - 1,)),
            pltpu.SemaphoreType.DMA((RING - 1,)),
            pltpu.SemaphoreType.DMA((2, RING + 1, 8)),
            pltpu.SemaphoreType.DMA((2, RING + 1, 8)),
            pltpu.SemaphoreType.DMA((2, 3)),
            pltpu.SemaphoreType.DMA((2, 3)),
            pltpu.SemaphoreType.DMA((RING - 1,)),
            pltpu.SemaphoreType.DMA((RING - 1,)),
            pltpu.SemaphoreType.DMA((20 * len(PIECES),)),
            pltpu.SemaphoreType.DMA((4, 2, 2, len(PIECES))),
            pltpu.SemaphoreType.DMA((2,)),
        ],
        compiler_params=pltpu.CompilerParams(
            collective_id=0, has_side_effects=True, vmem_limit_bytes=58 << 20
        ),
    )(
        tokens, cache_first, cache_second, gain_first, gain_second, gain_attn, conv_first, conv_second,
        query_weight, key_weight, value_weight, out_weight,
    )
    return jnp.swapaxes(out, 1, 2)


def solution(mesh):
    spread, kept = P("tm", "row", "col", None), P(None, "row", "col", None)
    return jax.shard_map(
        on_device,
        mesh=mesh,
        in_specs=(spread, kept, kept) + (P(),) * 9,
        out_specs=spread,
        check_vma=False,
    )
```

```python
import math

import jax
import jax.numpy as jnp
from jax import lax
from jax.experimental import pallas as pl
from jax.experimental.pallas import tpu as pltpu
from jax.sharding import PartitionSpec as P

MESH = pl.DeviceIdType.MESH
F32 = jnp.float32
BF16 = jnp.bfloat16
C, ROWS, COLS = 384, 16, 24
RING = 4
STRIP = COLS // RING
WIDE = STRIP + 2
CUT = STRIP * ROWS
PLACES = ROWS * COLS
PIECES = ((0, 2 * CUT), (2 * CUT, 2 * CUT))
LIFTED = 32
LANES = C // 128


def normed_by(v, gain):
    return v * lax.rsqrt(jnp.mean(v * v, axis=-1, keepdims=True) + 1e-06) * gain


def each(lo, hi, body, unroll):
    def step(n, _):
        body(n)
        return 0
    lax.fori_loop(lo, hi, step, 0, unroll=min(unroll, hi - lo))


def silu(v):
    return v / (1.0 + jnp.exp(-v))


def kernel(
    tok, cache1, cache2, gain1, gain2, gain_a, w1, w2, wq, wk, wv, wo,
    out,
    wbuf, views, lift, tok_t, raw, padded, lines_out, lines_in, corners_in, cache_in, made, final,
    normed, stream, blocks, query, mixed, top, total, mine, back,
    w_sem, cache_sem, ring_send, ring_recv, halo_send, halo_recv,
    past_send, past_recv, home_send, home_recv, attn_send, attn_recv, back_sem,
):
    nrow, ncol = lax.axis_size("row"), lax.axis_size("col")
    tm, row, col = (lax.axis_index(a) for a in ("tm", "row", "col"))
    x = lax.rem(tm, RING)
    ring = tm - x
    early = tm < RING
    strip = col * RING + x
    left_ok, right_ok = strip > 0, strip < ncol * RING - 1
    left = (jnp.where(x > 0, tm - 1, tm + RING - 1), row, jnp.where(x > 0, col, col - 1))
    right = (jnp.where(x < RING - 1, tm + 1, tm - RING + 1), row, jnp.where(x < RING - 1, col, col + 1))
    partner = (tm, row, lax.rem(col + 2, ncol))
    sibling = (tm, row, col + 1 - 2 * lax.rem(col, 2))
    up = (tm, lax.rem(row + 1, nrow), col)
    down = (tm, lax.rem(row + nrow - 1, nrow), col)

    def around(step):
        return lax.rem(x + step + RING, RING)

    @pl.when(jnp.logical_not(left_ok))
    def _():
        padded[:, :, 0] = jnp.zeros((2, 2 * RING + 2, ROWS, C), BF16)
        corners_in[:, :, :, 0] = jnp.zeros((2, RING + 1, 2, 16, C), BF16)

    @pl.when(jnp.logical_not(right_ok))
    def _():
        padded[:, :, WIDE - 1] = jnp.zeros((2, 2 * RING + 2, ROWS, C), BF16)
        corners_in[:, :, :, 1] = jnp.zeros((2, RING + 1, 2, 16, C), BF16)

    @pl.when(row == 0)
    def _():
        lines_in[:, :, 0] = jnp.zeros((2, RING + 1, 16, C), BF16)
        corners_in[:, :, 0] = jnp.zeros((2, RING + 1, 2, 16, C), BF16)

    @pl.when(row == nrow - 1)
    def _():
        lines_in[:, :, 1] = jnp.zeros((2, RING + 1, 16, C), BF16)
        corners_in[:, :, 1] = jnp.zeros((2, RING + 1, 2, 16, C), BF16)

    barrier = pltpu.get_barrier_semaphore()

    def greet(device):
        pl.semaphore_signal(barrier, inc=1, device_id=device, device_id_type=MESH)

    for step in range(1, RING):
        greet((ring + around(step), row, col))
    for device in (partner, sibling, up, down):
        greet(device)

    @pl.when(left_ok)
    def _():
        greet(left)

    @pl.when(right_ok)
    def _():
        greet(right)

    for ok, side in ((left_ok, left), (right_ok, right)):
        @pl.when(ok & (row > 0))
        def _():
            greet((side[0], row - 1, side[2]))

        @pl.when(ok & (row < nrow - 1))
        def _():
            greet((side[0], row + 1, side[2]))

    @pl.when(jnp.logical_not(early))
    def _():
        greet((tm - RING, row, col))

    def as_int(flag):
        return jnp.where(flag, 1, 0)

    beside = as_int(left_ok) + as_int(right_ok)
    above = as_int(row > 0) + as_int(row < nrow - 1)
    expected = RING - 1 + 4 + beside * (1 + above) + as_int(early)

    caches = [
        pltpu.make_async_copy(src, cache_in.at[stage], cache_sem.at[stage])
        for stage, src in ((0, cache1), (1, cache2))
    ]

    @pl.when(early)
    def _():
        for copy in caches:
            copy.start()

    weights = []
    for stage, src in ((0, w1), (1, w2)):
        for a in range(3):
            for c in range(3):
                copy = pltpu.make_async_copy(src.at[a, :, c], wbuf.at[stage, a, c], w_sem.at[stage])
                copy.start()
                weights.append((stage, copy))

    def wait_weights(stage):
        for s, copy in weights:
            if s == stage:
                copy.wait()

    lines = lift.reshape(LANES, COLS * LIFTED, 128)

    def put_line(at, v):
        for k in range(LANES):
            lines[k, pl.ds(8 + at, v.shape[0], stride=LIFTED), :] = v[:, k * 128:(k + 1) * 128]

    def get_line(at, count):
        return jnp.concatenate([
            lines[k, pl.ds(8 + at, count, stride=LIFTED), :] for k in range(LANES)
        ], axis=1)

    def put_column(j, v):
        for k in range(LANES):
            lift[k, j, 8:8 + ROWS, :] = v[:, k * 128:(k + 1) * 128]

    def get_column(j, at):
        return jnp.concatenate([lift[k, j, 8 + at:8 + at + ROWS, :] for k in range(LANES)], axis=1)

    def halo_copies(stage, p):
        frames = pl.ds(2 * p, 2)
        made = []

        def copy(ok, from_ok, src, dst, device):
            k = len(made)
            made.append((ok, from_ok, pltpu.make_async_remote_copy(
                src_ref=src, dst_ref=dst,
                send_sem=halo_send.at[stage, p, k], recv_sem=halo_recv.at[stage, p, k],
                device_id=device, device_id_type=MESH,
            )))

        for ok, from_ok, mine_at, theirs, device in (
            (left_ok, right_ok, 1, WIDE - 1, left), (right_ok, left_ok, WIDE - 2, 0, right)
        ):
            copy(ok, from_ok, padded.at[stage, frames, mine_at], padded.at[stage, frames, theirs], device)
        for n, (ok, from_ok, to_row) in enumerate((
            (row > 0, row < nrow - 1, row - 1), (row < nrow - 1, row > 0, row + 1)
        )):
            src = lines_out.at[stage, p, n]
            copy(ok, from_ok, src, lines_in.at[stage, p, 1 - n], (tm, to_row, col))
            copy(ok & left_ok, from_ok & right_ok, src, corners_in.at[stage, p, 1 - n, 1],
                 (left[0], to_row, left[2]))
            copy(ok & right_ok, from_ok & left_ok, src, corners_in.at[stage, p, 1 - n, 0],
                 (right[0], to_row, right[2]))
        return made

    def on(pairs, act):
        for ok, copy in pairs:
            @pl.when(ok)
            def _():
                act(copy)

    def start(copy):
        copy.start()

    def wait_recv(copy):
        copy.wait_recv()

    def wait_send(copy):
        copy.wait_send()

    def await_halo(stage, p):
        on([(from_ok, copy) for _, from_ok, copy in halo_copies(stage, p)], wait_recv)

    def send_halo(stage, p):
        def step(n):
            for i in range(2):
                put_column(WIDE * i + n, padded[stage, 2 * p + i, n].astype(F32))
        each(1, WIDE - 1, step, STRIP)
        for n, at in ((0, 0), (1, ROWS - 1)):
            lines_out[stage, p, n] = get_line(at, 2 * WIDE).astype(BF16)
        on([(ok, copy) for ok, _, copy in halo_copies(stage, p)], start)

    def build(stage, p):
        def up_step(n):
            for i in range(2):
                put_column(WIDE * i + n, padded[stage, 2 * p + i, n].astype(F32))
        each(0, WIDE, up_step, WIDE)
        for t, at in ((0, -1), (1, ROWS)):
            put_line(at, lines_in[stage, p, t].astype(F32))
            for lr, theirs, mine_at in ((0, WIDE - 2, 0), (1, 1, WIDE - 1)):
                v = corners_in[stage, p, t, lr].astype(F32)
                for i in range(2):
                    for k in range(LANES):
                        lift[k, WIDE * i + mine_at, 8 + at:9 + at, :] = (
                            v[WIDE * i + theirs:WIDE * i + theirs + 1, k * 128:(k + 1) * 128]
                        )

        def step(n):
            for i in range(2):
                for b in range(3):
                    views[2 * p + i, n, :, b * C:(b + 1) * C] = get_column(WIDE * i + n, b - 1).astype(BF16)
        each(0, WIDE, step, 4)

    def past_copies(stage):
        device = (tm + RING, row, col)
        return [
            pltpu.make_async_remote_copy(
                src_ref=src, dst_ref=dst,
                send_sem=past_send.at[stage, n], recv_sem=past_recv.at[stage, n],
                device_id=device, device_id_type=MESH,
            )
            for n, (src, dst) in enumerate((
                (padded.at[stage, pl.ds(2 * RING, 2)], padded.at[stage, pl.ds(0, 2)]),
                (lines_in.at[stage, RING], lines_in.at[stage, 0]),
                (corners_in.at[stage, RING], corners_in.at[stage, 0]),
            ))
        ]

    def send_past(stage):
        @pl.when(early)
        def _():
            for copy in past_copies(stage):
                copy.start()

    def build_past(stage):
        @pl.when(early)
        def _():
            await_halo(stage, 0)

        @pl.when(jnp.logical_not(early))
        def _():
            for copy in past_copies(stage):
                copy.wait_recv()
        build(stage, 0)

    def conv(stage, p):
        parts = [
            views[pl.ds(2 * p - 2 + a, 2), c:c + STRIP].reshape(2 * CUT, 3 * C)
            for a in range(3) for c in range(3)
        ]
        whole = jnp.concatenate(parts, axis=1)
        return jnp.dot(whole, wbuf[stage].reshape(27 * C, C), preferred_element_type=F32)

    for i in range(2):
        def turn(r):
            put_line(r, tok[i, r].astype(F32))
        each(0, ROWS, turn, 8)

        def settle(j):
            tok_t[i, j] = get_column(j, 0).astype(BF16)
        each(0, COLS, settle, 8)

    def ring_copy(step):
        return pltpu.make_async_remote_copy(
            src_ref=tok_t.at[:, pl.ds(STRIP * around(step), STRIP)],
            dst_ref=raw.at[pl.ds(2 * x, 2)],
            send_sem=ring_send.at[step - 1],
            recv_sem=ring_recv.at[step - 1],
            device_id=(ring + around(step), row, col),
            device_id_type=MESH,
        )

    pl.semaphore_wait(barrier, expected)
    for step in (2, 1, 3):
        ring_copy(step).start()

    @pl.when(early)
    def _():
        for stage in range(2):
            caches[stage].wait()
            for i in range(2):
                def turn(r):
                    put_line(r, cache_in[stage, i, r].astype(F32))
                each(0, ROWS, turn, 8)

                def settle(j):
                    padded[stage, i, 1 + j] = get_column(STRIP * x + j, 0).astype(BF16)
                each(0, STRIP, settle, 8)
            send_halo(stage, 0)

    def first(p):
        for i in range(2):
            def step(j):
                v = raw[2 * p - 2 + i, j].astype(F32)
                padded[0, 2 * p + i, 1 + j] = silu(normed_by(v, gain1[...])).astype(BF16)
            each(0, STRIP, step, STRIP)
        send_halo(0, p)

    raw[pl.ds(2 * x, 2)] = tok_t[:, pl.ds(STRIP * x, STRIP)]
    first(1 + x)

    for step in (1, 3, 2):
        ring_copy(step).wait_recv()
        first(1 + around(-step))
    order = tuple(range(RING, 0, -1))
    for p in order:
        await_halo(0, p)
        if p == RING:
            send_past(0)
        build(0, p)
    wait_weights(0)

    def follow(n):
        if 0 <= n < RING:
            await_halo(1, order[n])
            if order[n] == RING:
                send_past(1)
            build(1, order[n])

    for n, p in enumerate(order):
        if p == 1:
            build_past(0)
        made[...] = conv(0, p)

        def second(j):
            for i in range(2):
                v = made[pl.ds(pl.multiple_of(i * CUT + j * ROWS, ROWS), ROWS)]
                padded[1, 2 * p + i, 1 + j] = silu(normed_by(v, gain2[...])).astype(BF16)
        each(0, STRIP, second, STRIP)
        send_halo(1, p)
        follow(n - 2)
    follow(RING - 2)
    build_past(1)
    follow(RING - 1)
    wait_weights(1)

    frame = col // 2
    other = 1 - frame
    sent = []

    def send(src, dst, piece, device):
        rel, half, core = dst
        lo, size = PIECES[piece]
        copy = pltpu.make_async_remote_copy(
            src_ref=src.at[pl.ds(lo, size)],
            dst_ref=blocks.at[rel, half, core, pl.ds(lo, size)],
            send_sem=attn_send.at[len(sent)],
            recv_sem=attn_recv.at[rel, half, core, piece],
            device_id=device,
            device_id_type=MESH,
        )
        copy.start()
        sent.append(copy)

    def arrived(rel, half, core, piece):
        lo, size = PIECES[piece]
        ref = blocks.at[rel, half, core, pl.ds(lo, size)]
        pltpu.make_async_remote_copy(
            src_ref=ref, dst_ref=ref,
            send_sem=attn_send.at[0], recv_sem=attn_recv.at[rel, half, core, piece],
            device_id=partner, device_id_type=MESH,
        ).wait_recv()

    def home_copy(n):
        return pltpu.make_async_remote_copy(
            src_ref=final.at[n],
            dst_ref=stream.at[:, pl.ds(n * CUT, CUT)],
            send_sem=home_send.at[n],
            recv_sem=home_recv.at[n],
            device_id=(ring + around(n + 1), row, col),
            device_id_type=MESH,
        )

    def at_home(n):
        if n < RING - 1:
            home_copy(n).wait_recv()

        def step(j):
            for i in range(2):
                at = pl.ds(pl.multiple_of(n * CUT + j * ROWS, ROWS), ROWS)
                normed[i, at] = normed_by(stream[i, at].astype(F32), gain_a[...]).astype(BF16)
        each(0, STRIP, step, STRIP)

    def share(piece):
        send(normed.at[other], (0, 1, 0), piece, partner)
        send(normed.at[frame], (3, 0, 0), piece, up)
        send(normed.at[frame], (1, 0, 0), piece, down)
        send(normed.at[frame], (0, 0, 1), piece, sibling)

    for n in range(RING):
        p = 1 + around(n + 1)
        made[...] = conv(1, p)

        def last(j):
            for i in range(2):
                v = made[pl.ds(pl.multiple_of(i * CUT + j * ROWS, ROWS), ROWS)]
                v = (v + raw[2 * p - 2 + i, j].astype(F32)).astype(BF16)
                if n < RING - 1:
                    final[n, i, pl.ds(pl.multiple_of(j * ROWS, ROWS), ROWS)] = v
                else:
                    stream[i, pl.ds(pl.multiple_of(n * CUT + j * ROWS, ROWS), ROWS)] = v
        each(0, STRIP, last, STRIP)
        if n < RING - 1:
            home_copy(n).start()
        if n > 0:
            at_home(n - 1)
            if n == 2:
                share(0)
    at_home(RING - 1)
    share(1)

    blocks[0, 0, 0] = normed[frame]
    factor = math.log2(math.e) * C ** (-0.5)

    def ask(half):
        q = jnp.dot(blocks[0, half, 0], wq[...], preferred_element_type=F32).astype(BF16)
        q = lax.dot_general(wk[...], q, (((1,), (1,)), ((), ())), preferred_element_type=F32)
        query[:, half * PLACES:(half + 1) * PLACES] = (q * factor).astype(BF16)

    both, theirs = slice(0, 2 * PLACES), slice(PLACES, 2 * PLACES)

    def absorb(rel, half, at=both, initial=False):
        keys = blocks[rel, half].reshape(2 * PLACES, C)
        s = jnp.dot(keys, query[:, at], preferred_element_type=F32)
        now = jnp.max(s, axis=0, keepdims=True)
        if not initial:
            before = top[0:1, at]
            now = jnp.maximum(before, now)
            shrink = jnp.exp2(before - now)
        expo = jnp.exp2(s - now)
        summed = jnp.sum(expo, axis=0, keepdims=True)
        new = lax.dot_general(
            keys, expo.astype(BF16), (((0,), (0,)), ((), ())), preferred_element_type=F32
        )
        if initial:
            total[0:1, at] = summed
            mixed[:, at] = new
        else:
            total[0:1, at] = total[0:1, at] * shrink + summed
            mixed[:, at] = mixed[:, at] * shrink + new
        top[0:1, at] = now

    def relay(src, moves):
        for piece in range(len(PIECES)):
            arrived(*src, piece)
            for dst, device in moves:
                send(blocks.at[src], dst, piece, device)

    def ready(rel, half):
        for piece in range(len(PIECES)):
            arrived(rel, half, 1, piece)

    ask(0)
    relay((0, 1, 0), (((3, 1, 0), up), ((1, 1, 0), down), ((0, 1, 1), sibling)))
    ask(1)
    relay((3, 0, 0), (((2, 0, 0), up), ((3, 0, 1), sibling)))
    relay((1, 0, 0), (((1, 0, 1), sibling),))
    ready(0, 0)
    absorb(0, 0, both, True)
    ready(0, 1)
    absorb(0, 1)
    relay((3, 1, 0), (((3, 1, 1), sibling),))
    relay((1, 1, 0), (((2, 1, 0), down), ((1, 1, 1), sibling)))
    ready(3, 0)
    absorb(3, 0)
    ready(1, 0)
    absorb(1, 0)
    relay((2, 0, 0), (((2, 0, 1), sibling),))
    ready(3, 1)
    absorb(3, 1, theirs)
    relay((2, 1, 0), (((2, 1, 1), sibling),))
    ready(1, 1)
    absorb(1, 1, theirs)
    ready(2, 0)
    absorb(2, 0, theirs)
    ready(2, 1)
    absorb(2, 1, theirs)

    def attended(h):
        at = slice(h * PLACES, (h + 1) * PLACES)
        v = (mixed[:, at] / total[0:1, at]).T.astype(BF16)
        return jnp.dot(v, wv[...], preferred_element_type=F32).astype(BF16)

    def finish(i, values):
        v = stream[i].astype(F32) + jnp.dot(values, wo[...], preferred_element_type=F32)
        for n in range(RING):
            out[i, pl.ds(STRIP * around(-1 - n), STRIP)] = (
                v[n * CUT:(n + 1) * CUT].astype(BF16).reshape(STRIP, ROWS, C)
            )

    mine[...] = attended(1)
    copy = pltpu.make_async_remote_copy(
        src_ref=mine, dst_ref=back, send_sem=back_sem.at[0], recv_sem=back_sem.at[1],
        device_id=partner, device_id_type=MESH,
    )
    copy.start()
    for rel, half in ((3, 1), (1, 1), (2, 0), (2, 1)):
        absorb(rel, half, slice(0, PLACES))
    own = attended(0)
    finish(frame, own)
    copy.wait()
    finish(other, back[...])

    for copy in sent:
        copy.wait_send()
    for step in range(1, RING):
        ring_copy(step).wait_send()
        home_copy(step - 1).wait_send()
    for stage in range(2):
        for p in range(RING + 1):
            on([(ok & early if p == 0 else ok, copy) for ok, _, copy in halo_copies(stage, p)], wait_send)

        @pl.when(early)
        def _():
            for copy in past_copies(stage):
                copy.wait_send()


def on_device(
    tokens, cache_first, cache_second, gain_first, gain_second, conv_first, conv_second,
    gain_attn, query_weight, key_weight, value_weight, out_weight,
):
    vmem = pl.BlockSpec(memory_space=pltpu.VMEM)
    hbm = pl.BlockSpec(memory_space=pl.ANY)
    pair = (2, RING + 1, 2)
    out = pl.pallas_call(
        kernel,
        out_shape=jax.ShapeDtypeStruct((2, COLS, ROWS, C), BF16),
        in_specs=[vmem, hbm, hbm, vmem, vmem, vmem, hbm, hbm, vmem, vmem, vmem, vmem],
        out_specs=vmem,
        scratch_shapes=[
            pltpu.VMEM((2, 3, 3, 3, C, C), BF16),
            pltpu.VMEM((2 * RING + 2, WIDE, ROWS, 3 * C), BF16),
            pltpu.VMEM((LANES, COLS, LIFTED, 128), F32),
            pltpu.VMEM((2, COLS, ROWS, C), BF16),
            pltpu.VMEM((2 * RING, STRIP, ROWS, C), BF16),
            pltpu.VMEM((2, 2 * RING + 2, WIDE, ROWS, C), BF16),
            pltpu.VMEM(pair + (16, C), BF16),
            pltpu.VMEM(pair + (16, C), BF16),
            pltpu.VMEM(pair + (2, 16, C), BF16),
            pltpu.VMEM((2, 2, ROWS, COLS, C), BF16),
            pltpu.VMEM((2 * CUT, C), F32),
            pltpu.VMEM((RING - 1, 2, CUT, C), BF16),
            pltpu.VMEM((2, PLACES, C), BF16),
            pltpu.VMEM((2, PLACES, C), BF16),
            pltpu.VMEM((4, 2, 2, PLACES, C), BF16),
            pltpu.VMEM((C, 2 * PLACES), BF16),
            pltpu.VMEM((C, 2 * PLACES), F32),
            pltpu.VMEM((8, 2 * PLACES), F32),
            pltpu.VMEM((8, 2 * PLACES), F32),
            pltpu.VMEM((PLACES, C), BF16),
            pltpu.VMEM((PLACES, C), BF16),
            pltpu.SemaphoreType.DMA((2,)),
            pltpu.SemaphoreType.DMA((2,)),
            pltpu.SemaphoreType.DMA((RING - 1,)),
            pltpu.SemaphoreType.DMA((RING - 1,)),
            pltpu.SemaphoreType.DMA((2, RING + 1, 8)),
            pltpu.SemaphoreType.DMA((2, RING + 1, 8)),
            pltpu.SemaphoreType.DMA((2, 3)),
            pltpu.SemaphoreType.DMA((2, 3)),
            pltpu.SemaphoreType.DMA((RING - 1,)),
            pltpu.SemaphoreType.DMA((RING - 1,)),
            pltpu.SemaphoreType.DMA((20 * len(PIECES),)),
            pltpu.SemaphoreType.DMA((4, 2, 2, len(PIECES))),
            pltpu.SemaphoreType.DMA((2,)),
        ],
        compiler_params=pltpu.CompilerParams(
            collective_id=0, has_side_effects=True, vmem_limit_bytes=58 << 20
        ),
    )(
        tokens, cache_first, cache_second, gain_first, gain_second, gain_attn, conv_first, conv_second,
        query_weight, key_weight, value_weight, out_weight,
    )
    return jnp.swapaxes(out, 1, 2)


def solution(mesh):
    spread, kept = P("tm", "row", "col", None), P(None, "row", "col", None)
    return jax.shard_map(
        on_device,
        mesh=mesh,
        in_specs=(spread, kept, kept) + (P(),) * 9,
        out_specs=spread,
        check_vma=False,
    )
```

```python
import math

import jax
import jax.numpy as jnp
from jax import lax
from jax.experimental import pallas as pl
from jax.experimental.pallas import tpu as pltpu
from jax.sharding import PartitionSpec as P

MESH = pl.DeviceIdType.MESH
F32 = jnp.float32
BF16 = jnp.bfloat16
C, ROWS, COLS = 384, 16, 24
RING = 4
STRIP = COLS // RING
WIDE = STRIP + 2
CUT = STRIP * ROWS
PLACES = ROWS * COLS
PIECES = ((0, 2 * CUT), (2 * CUT, 2 * CUT))
LIFTED = 32
LANES = C // 128


def normed_by(v, gain):
    return v * lax.rsqrt(jnp.mean(v * v, axis=-1, keepdims=True) + 1e-06) * gain


def each(lo, hi, body, unroll):
    def step(n, _):
        body(n)
        return 0
    lax.fori_loop(lo, hi, step, 0, unroll=min(unroll, hi - lo))


def silu(v):
    return v / (1.0 + jnp.exp(-v))


def kernel(
    tok, cache1, cache2, gain1, gain2, gain_a, w1, w2, wq, wk, wv, wo,
    out,
    wbuf, views, lift, tok_t, raw, padded, lines_out, lines_in, corners_in, cache_in, made, final,
    normed, stream, blocks, query, mixed, top, total, mine, back,
    w_sem, cache_sem, ring_send, ring_recv, halo_send, halo_recv,
    past_send, past_recv, home_send, home_recv, attn_send, attn_recv, back_sem,
):
    nrow, ncol = lax.axis_size("row"), lax.axis_size("col")
    tm, row, col = (lax.axis_index(a) for a in ("tm", "row", "col"))
    x = lax.rem(tm, RING)
    ring = tm - x
    early = tm < RING
    strip = col * RING + x
    left_ok, right_ok = strip > 0, strip < ncol * RING - 1
    left = (jnp.where(x > 0, tm - 1, tm + RING - 1), row, jnp.where(x > 0, col, col - 1))
    right = (jnp.where(x < RING - 1, tm + 1, tm - RING + 1), row, jnp.where(x < RING - 1, col, col + 1))
    partner = (tm, row, lax.rem(col + 2, ncol))
    sibling = (tm, row, col + 1 - 2 * lax.rem(col, 2))
    up = (tm, lax.rem(row + 1, nrow), col)
    down = (tm, lax.rem(row + nrow - 1, nrow), col)

    def around(step):
        return lax.rem(x + step + RING, RING)

    @pl.when(jnp.logical_not(left_ok))
    def _():
        padded[:, :, 0] = jnp.zeros((2, 2 * RING + 2, ROWS, C), BF16)
        corners_in[:, :, :, 0] = jnp.zeros((2, RING + 1, 2, 16, C), BF16)

    @pl.when(jnp.logical_not(right_ok))
    def _():
        padded[:, :, WIDE - 1] = jnp.zeros((2, 2 * RING + 2, ROWS, C), BF16)
        corners_in[:, :, :, 1] = jnp.zeros((2, RING + 1, 2, 16, C), BF16)

    @pl.when(row == 0)
    def _():
        lines_in[:, :, 0] = jnp.zeros((2, RING + 1, 16, C), BF16)
        corners_in[:, :, 0] = jnp.zeros((2, RING + 1, 2, 16, C), BF16)

    @pl.when(row == nrow - 1)
    def _():
        lines_in[:, :, 1] = jnp.zeros((2, RING + 1, 16, C), BF16)
        corners_in[:, :, 1] = jnp.zeros((2, RING + 1, 2, 16, C), BF16)

    barrier = pltpu.get_barrier_semaphore()

    def greet(device):
        pl.semaphore_signal(barrier, inc=1, device_id=device, device_id_type=MESH)

    for step in range(1, RING):
        greet((ring + around(step), row, col))
    for device in (partner, sibling, up, down):
        greet(device)

    @pl.when(left_ok)
    def _():
        greet(left)

    @pl.when(right_ok)
    def _():
        greet(right)

    for ok, side in ((left_ok, left), (right_ok, right)):
        @pl.when(ok & (row > 0))
        def _():
            greet((side[0], row - 1, side[2]))

        @pl.when(ok & (row < nrow - 1))
        def _():
            greet((side[0], row + 1, side[2]))

    @pl.when(jnp.logical_not(early))
    def _():
        greet((tm - RING, row, col))

    def as_int(flag):
        return jnp.where(flag, 1, 0)

    beside = as_int(left_ok) + as_int(right_ok)
    above = as_int(row > 0) + as_int(row < nrow - 1)
    expected = RING - 1 + 4 + beside * (1 + above) + as_int(early)

    caches = [
        pltpu.make_async_copy(src, cache_in.at[stage], cache_sem.at[stage])
        for stage, src in ((0, cache1), (1, cache2))
    ]

    @pl.when(early)
    def _():
        for copy in caches:
            copy.start()

    weights = []
    for stage, src in ((0, w1), (1, w2)):
        for a in range(3):
            for c in range(3):
                copy = pltpu.make_async_copy(src.at[a, :, c], wbuf.at[stage, a, c], w_sem.at[stage])
                copy.start()
                weights.append((stage, copy))

    def wait_weights(stage):
        for s, copy in weights:
            if s == stage:
                copy.wait()

    lines = lift.reshape(LANES, COLS * LIFTED, 128)

    def put_line(at, v):
        for k in range(LANES):
            lines[k, pl.ds(8 + at, v.shape[0], stride=LIFTED), :] = v[:, k * 128:(k + 1) * 128]

    def get_line(at, count):
        return jnp.concatenate([
            lines[k, pl.ds(8 + at, count, stride=LIFTED), :] for k in range(LANES)
        ], axis=1)

    def put_column(j, v):
        for k in range(LANES):
            lift[k, j, 8:8 + ROWS, :] = v[:, k * 128:(k + 1) * 128]

    def get_column(j, at):
        return jnp.concatenate([lift[k, j, 8 + at:8 + at + ROWS, :] for k in range(LANES)], axis=1)

    def halo_copies(stage, p):
        frames = pl.ds(2 * p, 2)
        made = []

        def copy(ok, from_ok, src, dst, device):
            k = len(made)
            made.append((ok, from_ok, pltpu.make_async_remote_copy(
                src_ref=src, dst_ref=dst,
                send_sem=halo_send.at[stage, p, k], recv_sem=halo_recv.at[stage, p, k],
                device_id=device, device_id_type=MESH,
            )))

        for ok, from_ok, mine_at, theirs, device in (
            (left_ok, right_ok, 1, WIDE - 1, left), (right_ok, left_ok, WIDE - 2, 0, right)
        ):
            copy(ok, from_ok, padded.at[stage, frames, mine_at], padded.at[stage, frames, theirs], device)
        for n, (ok, from_ok, to_row) in enumerate((
            (row > 0, row < nrow - 1, row - 1), (row < nrow - 1, row > 0, row + 1)
        )):
            src = lines_out.at[stage, p, n]
            copy(ok, from_ok, src, lines_in.at[stage, p, 1 - n], (tm, to_row, col))
            copy(ok & left_ok, from_ok & right_ok, src, corners_in.at[stage, p, 1 - n, 1],
                 (left[0], to_row, left[2]))
            copy(ok & right_ok, from_ok & left_ok, src, corners_in.at[stage, p, 1 - n, 0],
                 (right[0], to_row, right[2]))
        return made

    def on(pairs, act):
        for ok, copy in pairs:
            @pl.when(ok)
            def _():
                act(copy)

    def start(copy):
        copy.start()

    def wait_recv(copy):
        copy.wait_recv()

    def wait_send(copy):
        copy.wait_send()

    def await_halo(stage, p):
        on([(from_ok, copy) for _, from_ok, copy in halo_copies(stage, p)], wait_recv)

    def send_halo(stage, p):
        def step(n):
            for i in range(2):
                put_column(WIDE * i + n, padded[stage, 2 * p + i, n].astype(F32))
        each(1, WIDE - 1, step, STRIP)
        for n, at in ((0, 0), (1, ROWS - 1)):
            lines_out[stage, p, n] = get_line(at, 2 * WIDE).astype(BF16)
        on([(ok, copy) for ok, _, copy in halo_copies(stage, p)], start)

    def build(stage, p):
        def up_step(n):
            for i in range(2):
                put_column(WIDE * i + n, padded[stage, 2 * p + i, n].astype(F32))
        each(0, WIDE, up_step, WIDE)
        for t, at in ((0, -1), (1, ROWS)):
            put_line(at, lines_in[stage, p, t].astype(F32))
            for lr, theirs, mine_at in ((0, WIDE - 2, 0), (1, 1, WIDE - 1)):
                v = corners_in[stage, p, t, lr].astype(F32)
                for i in range(2):
                    for k in range(LANES):
                        lift[k, WIDE * i + mine_at, 8 + at:9 + at, :] = (
                            v[WIDE * i + theirs:WIDE * i + theirs + 1, k * 128:(k + 1) * 128]
                        )

        def step(n):
            for i in range(2):
                for b in range(3):
                    views[2 * p + i, n, :, b * C:(b + 1) * C] = get_column(WIDE * i + n, b - 1).astype(BF16)
        each(0, WIDE, step, 4)

    def past_copies(stage):
        device = (tm + RING, row, col)
        return [
            pltpu.make_async_remote_copy(
                src_ref=src, dst_ref=dst,
                send_sem=past_send.at[stage, n], recv_sem=past_recv.at[stage, n],
                device_id=device, device_id_type=MESH,
            )
            for n, (src, dst) in enumerate((
                (padded.at[stage, pl.ds(2 * RING, 2)], padded.at[stage, pl.ds(0, 2)]),
                (lines_in.at[stage, RING], lines_in.at[stage, 0]),
                (corners_in.at[stage, RING], corners_in.at[stage, 0]),
            ))
        ]

    def send_past(stage):
        @pl.when(early)
        def _():
            for copy in past_copies(stage):
                copy.start()

    def build_past(stage):
        @pl.when(early)
        def _():
            await_halo(stage, 0)

        @pl.when(jnp.logical_not(early))
        def _():
            for copy in past_copies(stage):
                copy.wait_recv()
        build(stage, 0)

    def conv(stage, p):
        parts = [
            views[pl.ds(2 * p - 2 + a, 2), c:c + STRIP].reshape(2 * CUT, 3 * C)
            for a in range(3) for c in range(3)
        ]
        whole = jnp.concatenate(parts, axis=1)
        return jnp.dot(whole, wbuf[stage].reshape(27 * C, C), preferred_element_type=F32)

    for i in range(2):
        def turn(r):
            put_line(r, tok[i, r].astype(F32))
        each(0, ROWS, turn, 8)

        def settle(j):
            tok_t[i, j] = get_column(j, 0).astype(BF16)
        each(0, COLS, settle, 8)

    def ring_copy(step):
        return pltpu.make_async_remote_copy(
            src_ref=tok_t.at[:, pl.ds(STRIP * around(step), STRIP)],
            dst_ref=raw.at[pl.ds(2 * x, 2)],
            send_sem=ring_send.at[step - 1],
            recv_sem=ring_recv.at[step - 1],
            device_id=(ring + around(step), row, col),
            device_id_type=MESH,
        )

    pl.semaphore_wait(barrier, expected)
    for step in (2, 1, 3):
        ring_copy(step).start()

    @pl.when(early)
    def _():
        for stage in range(2):
            caches[stage].wait()
            for i in range(2):
                def turn(r):
                    put_line(r, cache_in[stage, i, r].astype(F32))
                each(0, ROWS, turn, 8)

                def settle(j):
                    padded[stage, i, 1 + j] = get_column(STRIP * x + j, 0).astype(BF16)
                each(0, STRIP, settle, 8)
            send_halo(stage, 0)

    def first(p):
        for i in range(2):
            def step(j):
                v = raw[2 * p - 2 + i, j].astype(F32)
                padded[0, 2 * p + i, 1 + j] = silu(normed_by(v, gain1[...])).astype(BF16)
            each(0, STRIP, step, STRIP)
        send_halo(0, p)

    raw[pl.ds(2 * x, 2)] = tok_t[:, pl.ds(STRIP * x, STRIP)]
    first(1 + x)

    for step in (1, 3, 2):
        ring_copy(step).wait_recv()
        first(1 + around(-step))
    order = tuple(range(RING, 0, -1))
    for p in order:
        await_halo(0, p)
        if p == RING:
            send_past(0)
        build(0, p)
    wait_weights(0)

    def follow(n):
        if 0 <= n < RING:
            await_halo(1, order[n])
            if order[n] == RING:
                send_past(1)
            build(1, order[n])

    for n, p in enumerate(order):
        if p == 1:
            build_past(0)
        made[...] = conv(0, p)

        def second(j):
            for i in range(2):
                v = made[pl.ds(pl.multiple_of(i * CUT + j * ROWS, ROWS), ROWS)]
                padded[1, 2 * p + i, 1 + j] = silu(normed_by(v, gain2[...])).astype(BF16)
        each(0, STRIP, second, STRIP)
        send_halo(1, p)
        follow(n - 2)
    follow(RING - 2)
    build_past(1)
    follow(RING - 1)
    wait_weights(1)

    frame = col // 2
    other = 1 - frame
    sent = []

    def send(src, dst, piece, device):
        rel, half, core = dst
        lo, size = PIECES[piece]
        copy = pltpu.make_async_remote_copy(
            src_ref=src.at[pl.ds(lo, size)],
            dst_ref=blocks.at[rel, half, core, pl.ds(lo, size)],
            send_sem=attn_send.at[len(sent)],
            recv_sem=attn_recv.at[rel, half, core, piece],
            device_id=device,
            device_id_type=MESH,
        )
        copy.start()
        sent.append(copy)

    def arrived(rel, half, core, piece):
        lo, size = PIECES[piece]
        ref = blocks.at[rel, half, core, pl.ds(lo, size)]
        pltpu.make_async_remote_copy(
            src_ref=ref, dst_ref=ref,
            send_sem=attn_send.at[0], recv_sem=attn_recv.at[rel, half, core, piece],
            device_id=partner, device_id_type=MESH,
        ).wait_recv()

    def home_copy(n):
        return pltpu.make_async_remote_copy(
            src_ref=final.at[n],
            dst_ref=stream.at[:, pl.ds(n * CUT, CUT)],
            send_sem=home_send.at[n],
            recv_sem=home_recv.at[n],
            device_id=(ring + around(n + 1), row, col),
            device_id_type=MESH,
        )

    def at_home(n):
        if n < RING - 1:
            home_copy(n).wait_recv()

        def step(j):
            for i in range(2):
                at = pl.ds(pl.multiple_of(n * CUT + j * ROWS, ROWS), ROWS)
                normed[i, at] = normed_by(stream[i, at].astype(F32), gain_a[...]).astype(BF16)
        each(0, STRIP, step, STRIP)

    def share(piece):
        send(normed.at[other], (0, 1, 0), piece, partner)
        send(normed.at[frame], (3, 0, 0), piece, up)
        send(normed.at[frame], (1, 0, 0), piece, down)
        send(normed.at[frame], (0, 0, 1), piece, sibling)

    for n in range(RING):
        p = 1 + around(n + 1)
        made[...] = conv(1, p)

        def last(j):
            for i in range(2):
                v = made[pl.ds(pl.multiple_of(i * CUT + j * ROWS, ROWS), ROWS)]
                v = (v + raw[2 * p - 2 + i, j].astype(F32)).astype(BF16)
                if n < RING - 1:
                    final[n, i, pl.ds(pl.multiple_of(j * ROWS, ROWS), ROWS)] = v
                else:
                    stream[i, pl.ds(pl.multiple_of(n * CUT + j * ROWS, ROWS), ROWS)] = v
        each(0, STRIP, last, STRIP)
        if n < RING - 1:
            home_copy(n).start()
        if n > 0:
            at_home(n - 1)
            if n == 2:
                share(0)
    at_home(RING - 1)
    share(1)

    blocks[0, 0, 0] = normed[frame]
    factor = math.log2(math.e) * C ** (-0.5)

    def ask(half):
        q = jnp.dot(blocks[0, half, 0], wq[...], preferred_element_type=F32).astype(BF16)
        q = lax.dot_general(wk[...], q, (((1,), (1,)), ((), ())), preferred_element_type=F32)
        query[:, half * PLACES:(half + 1) * PLACES] = (q * factor).astype(BF16)

    both, theirs = slice(0, 2 * PLACES), slice(PLACES, 2 * PLACES)

    def absorb(rel, half, at=both, initial=False):
        if half is None:
            keys = blocks[rel].reshape(4 * PLACES, C)
        else:
            keys = blocks[rel, half].reshape(2 * PLACES, C)
        s = jnp.dot(keys, query[:, at], preferred_element_type=F32)
        now = jnp.max(s, axis=0, keepdims=True)
        if not initial:
            before = top[0:1, at]
            now = jnp.maximum(before, now)
            shrink = jnp.exp2(before - now)
        expo = jnp.exp2(s - now)
        summed = jnp.sum(expo, axis=0, keepdims=True)
        new = lax.dot_general(
            keys, expo.astype(BF16), (((0,), (0,)), ((), ())), preferred_element_type=F32
        )
        if initial:
            total[0:1, at] = summed
            mixed[:, at] = new
        else:
            total[0:1, at] = total[0:1, at] * shrink + summed
            mixed[:, at] = mixed[:, at] * shrink + new
        top[0:1, at] = now

    def relay(src, moves):
        for piece in range(len(PIECES)):
            arrived(*src, piece)
            for dst, device in moves:
                send(blocks.at[src], dst, piece, device)

    def ready(rel, half):
        for piece in range(len(PIECES)):
            arrived(rel, half, 1, piece)

    ask(0)
    relay((0, 1, 0), (((3, 1, 0), up), ((1, 1, 0), down), ((0, 1, 1), sibling)))
    ask(1)
    relay((3, 0, 0), (((2, 0, 0), up), ((3, 0, 1), sibling)))
    relay((1, 0, 0), (((1, 0, 1), sibling),))
    ready(0, 0)
    absorb(0, 0, both, True)
    ready(0, 1)
    absorb(0, 1)
    relay((3, 1, 0), (((3, 1, 1), sibling),))
    relay((1, 1, 0), (((2, 1, 0), down), ((1, 1, 1), sibling)))
    ready(3, 0)
    absorb(3, 0, theirs)
    ready(1, 0)
    absorb(1, 0, theirs)
    relay((2, 0, 0), (((2, 0, 1), sibling),))
    ready(3, 1)
    absorb(3, 1, theirs)
    relay((2, 1, 0), (((2, 1, 1), sibling),))
    ready(1, 1)
    absorb(1, 1, theirs)
    ready(2, 0)
    absorb(2, 0, theirs)
    ready(2, 1)
    absorb(2, 1, theirs)

    def attended(h):
        at = slice(h * PLACES, (h + 1) * PLACES)
        v = (mixed[:, at] / total[0:1, at]).T.astype(BF16)
        return jnp.dot(v, wv[...], preferred_element_type=F32).astype(BF16)

    def finish(i, values):
        v = stream[i].astype(F32) + jnp.dot(values, wo[...], preferred_element_type=F32)
        for n in range(RING):
            out[i, pl.ds(STRIP * around(-1 - n), STRIP)] = (
                v[n * CUT:(n + 1) * CUT].astype(BF16).reshape(STRIP, ROWS, C)
            )

    mine[...] = attended(1)
    copy = pltpu.make_async_remote_copy(
        src_ref=mine, dst_ref=back, send_sem=back_sem.at[0], recv_sem=back_sem.at[1],
        device_id=partner, device_id_type=MESH,
    )
    copy.start()
    for rel in (3, 1, 2):
        absorb(rel, None, slice(0, PLACES))
    own = attended(0)
    finish(frame, own)
    copy.wait()
    finish(other, back[...])

    for copy in sent:
        copy.wait_send()
    for step in range(1, RING):
        ring_copy(step).wait_send()
        home_copy(step - 1).wait_send()
    for stage in range(2):
        for p in range(RING + 1):
            on([(ok & early if p == 0 else ok, copy) for ok, _, copy in halo_copies(stage, p)], wait_send)

        @pl.when(early)
        def _():
            for copy in past_copies(stage):
                copy.wait_send()


def on_device(
    tokens, cache_first, cache_second, gain_first, gain_second, conv_first, conv_second,
    gain_attn, query_weight, key_weight, value_weight, out_weight,
):
    vmem = pl.BlockSpec(memory_space=pltpu.VMEM)
    hbm = pl.BlockSpec(memory_space=pl.ANY)
    pair = (2, RING + 1, 2)
    out = pl.pallas_call(
        kernel,
        out_shape=jax.ShapeDtypeStruct((2, COLS, ROWS, C), BF16),
        in_specs=[vmem, hbm, hbm, vmem, vmem, vmem, hbm, hbm, vmem, vmem, vmem, vmem],
        out_specs=vmem,
        scratch_shapes=[
            pltpu.VMEM((2, 3, 3, 3, C, C), BF16),
            pltpu.VMEM((2 * RING + 2, WIDE, ROWS, 3 * C), BF16),
            pltpu.VMEM((LANES, COLS, LIFTED, 128), F32),
            pltpu.VMEM((2, COLS, ROWS, C), BF16),
            pltpu.VMEM((2 * RING, STRIP, ROWS, C), BF16),
            pltpu.VMEM((2, 2 * RING + 2, WIDE, ROWS, C), BF16),
            pltpu.VMEM(pair + (16, C), BF16),
            pltpu.VMEM(pair + (16, C), BF16),
            pltpu.VMEM(pair + (2, 16, C), BF16),
            pltpu.VMEM((2, 2, ROWS, COLS, C), BF16),
            pltpu.VMEM((2 * CUT, C), F32),
            pltpu.VMEM((RING - 1, 2, CUT, C), BF16),
            pltpu.VMEM((2, PLACES, C), BF16),
            pltpu.VMEM((2, PLACES, C), BF16),
            pltpu.VMEM((4, 2, 2, PLACES, C), BF16),
            pltpu.VMEM((C, 2 * PLACES), BF16),
            pltpu.VMEM((C, 2 * PLACES), F32),
            pltpu.VMEM((8, 2 * PLACES), F32),
            pltpu.VMEM((8, 2 * PLACES), F32),
            pltpu.VMEM((PLACES, C), BF16),
            pltpu.VMEM((PLACES, C), BF16),
            pltpu.SemaphoreType.DMA((2,)),
            pltpu.SemaphoreType.DMA((2,)),
            pltpu.SemaphoreType.DMA((RING - 1,)),
            pltpu.SemaphoreType.DMA((RING - 1,)),
            pltpu.SemaphoreType.DMA((2, RING + 1, 8)),
            pltpu.SemaphoreType.DMA((2, RING + 1, 8)),
            pltpu.SemaphoreType.DMA((2, 3)),
            pltpu.SemaphoreType.DMA((2, 3)),
            pltpu.SemaphoreType.DMA((RING - 1,)),
            pltpu.SemaphoreType.DMA((RING - 1,)),
            pltpu.SemaphoreType.DMA((20 * len(PIECES),)),
            pltpu.SemaphoreType.DMA((4, 2, 2, len(PIECES))),
            pltpu.SemaphoreType.DMA((2,)),
        ],
        compiler_params=pltpu.CompilerParams(
            collective_id=0, has_side_effects=True, vmem_limit_bytes=58 << 20
        ),
    )(
        tokens, cache_first, cache_second, gain_first, gain_second, gain_attn, conv_first, conv_second,
        query_weight, key_weight, value_weight, out_weight,
    )
    return jnp.swapaxes(out, 1, 2)


def solution(mesh):
    spread, kept = P("tm", "row", "col", None), P(None, "row", "col", None)
    return jax.shard_map(
        on_device,
        mesh=mesh,
        in_specs=(spread, kept, kept) + (P(),) * 9,
        out_specs=spread,
        check_vma=False,
    )
```
